128 devices in a mesh: session: 8 (over y, core), item: 16 (over x, z).
Axes of the slice: x: 4, y: 4, z: 4, core: 2. Of those that a mesh axis runs over, the one named last changes fastest.
Arguments:
- cache: bfloat16 [32, 4096, 2, 512], P('session', 'item'), may hold values from -6 to 6
- lengths: int32 [32], P('session'), may hold values from 512 to 4096
- new_slot: int32 [32], P('session'), may hold values from 0 to 31, as said below
- unique_ids: int32 [8, 5120], P('session', 'item'), may hold values from 0 to 1048575, as said below
- inverse: int32 [32, 4096], P('session', 'item'), may hold values from 0 to 319, as said below
- table: bfloat16 [1048576, 512], P(('session', 'item')), may hold values from -6 to 6
- w_qu: bfloat16 [512, 1024], replicated, may hold values from -0.25 to 0.25
- w_out: bfloat16 [512, 512], replicated, may hold values from -0.25 to 0.25
- w_head: bfloat16 [512], replicated, may hold values from -0.25 to 0.25
Outputs:
- migrated_cache: bfloat16 [32, 4096, 2, 512], P('session', 'item')
- scores: float32 [32, 4096], P('session', 'item')
The draws below stay inside these ranges and needn't reach their ends.
Inputs may be any that keep to these rules, and one draw needn't show every extreme that they name: `new_slot`: A permutation of the session slots; the owner of slot g is g // 4; no two sessions of one owner move to the same owner. `unique_ids`: each device's block of 320 entries holds distinct ids; id v lives on device v // 8192 of session+item. In every block each device is named 1 to 4 times, each of these four counts by a quarter of the devices. `inverse`: indexes the same device's block of unique_ids; every entry of a block is used.
All inputs are finite; a program needn't handle non-finite values.
Results may differ from the reference program's by a relative error of at most 0.003.
Values may be sent and summed in bfloat16 or wider, within the bound.
A program may use at most 192 MiB of HBM per device.

```python
import math
import jax
import jax.numpy as jnp
import numpy as np
from jax import lax

D = 512
HEADS = 4
SESS = 4
HIST = 4096
NCD = 256
ITEMS_DEV = 8192
ITEMS = 1048576
U = 320
G = 32
N_SESSION = 8
N_ITEM = 16
DEVICES = 128


def draw_new_slot(key, part):
    key = jax.random.fold_in(key, 1)
    second, third = jax.random.split(key, 2)
    shuffled = jax.random.permutation(second, N_SESSION).astype(jnp.int32)
    position = jnp.argsort(shuffled, stable=True).astype(jnp.int32)
    values = jnp.arange(N_SESSION, dtype=jnp.int32)
    priority = jnp.where(values == 1, -2, jnp.where(values == N_SESSION // 2, -1, position))
    offsets = jnp.argsort(priority, stable=True).astype(jnp.int32)[:SESS]
    orders = jax.vmap(lambda k: jax.random.permutation(k, SESS).astype(jnp.int32))(jax.random.split(third, N_SESSION))
    owner = jnp.arange(N_SESSION, dtype=jnp.int32)[:, None]
    target = (owner + offsets[None, :]) % N_SESSION
    local = orders[target, jnp.arange(SESS, dtype=jnp.int32)[None, :]]
    return (target * SESS + local).reshape(-1).astype(jnp.int32)


def draw_unique_ids(key, part):
    key = jax.random.fold_in(key, 2)
    base = jnp.asarray(np.repeat(np.arange(DEVICES), 1 + np.arange(DEVICES) % 4), jnp.int32)

    def one_device(device_key):
        first, second, third = jax.random.split(device_key, 3)
        relabel = jax.random.permutation(first, DEVICES).astype(jnp.int32)
        holder = relabel[base]
        rows = jax.random.permutation(second, ITEMS_DEV).astype(jnp.int32)[:U]
        ids = holder * ITEMS_DEV + rows
        order = jax.random.permutation(third, U)
        return ids[order]
    blocks = jax.vmap(one_device)(jax.random.split(key, DEVICES))
    return blocks.reshape(N_SESSION, N_ITEM * U).astype(jnp.int32)


def draw_inverse(key, part):
    key = jax.random.fold_in(key, 3)

    def one_device(device_key):
        first, second = jax.random.split(device_key)
        extra = jax.random.randint(first, (SESS * NCD - U,), 0, U, dtype=jnp.int32)
        values = jnp.concatenate([jnp.arange(U, dtype=jnp.int32), extra])
        order = jax.random.permutation(second, SESS * NCD)
        return values[order].reshape(SESS, NCD)
    blocks = jax.vmap(one_device)(jax.random.split(key, DEVICES))
    blocks = blocks.reshape(N_SESSION, N_ITEM, SESS, NCD).transpose(0, 2, 1, 3)
    return blocks.reshape(SESS * N_SESSION, NCD * N_ITEM).astype(jnp.int32)


def touch_ends(array, key, low, high):
    longest = array.shape.index(max(array.shape))
    spots = []
    for shift in (0, 1):
        where = [jax.random.randint(jax.random.fold_in(key, axis), (), 0, length) for axis, length in enumerate(array.shape)]
        where[longest] = (where[longest] + shift) % array.shape[longest]
        spots.append(tuple(where))
    return array.at[spots[0]].set(low).at[spots[1]].set(high)


def levels(stream_key, extent, cuts, low, largest):
    def one(dim, parts):
        steps = jax.random.uniform(jax.random.fold_in(jax.random.fold_in(stream_key, 6), dim), (parts,), jnp.float32, low / len(cuts), largest / len(cuts))
        return jnp.repeat(jnp.exp(steps), extent[dim] // parts).reshape((-1,) + (1,) * (len(extent) - dim - 1))

    factor_of = one(*cuts[0])
    for cut in cuts[1:]:
        factor_of = factor_of * one(*cut)
    return factor_of


def noise(stream_key, shape, scale, reach, pieces=(), kind=jnp.bfloat16):
    array = jax.random.normal(stream_key, shape, jnp.float32) * scale
    if len(pieces) > 0:
        array = levels(stream_key, shape, pieces, -0.22, 0.18) * array
    return jnp.clip(array, min=-reach, max=reach).astype(kind)


def setup_inputs(seed: int = 0) -> dict:
    key_list = jax.random.split(jax.random.key(seed), 10)
    cache = noise(key_list[0], (G, HIST, 2, D), 1.0, 6.0, ((0, 8), (1, 16)))
    lengths = touch_ends(jax.random.randint(key_list[1], (G,), HIST // 8, HIST + 1), jax.random.fold_in(key_list[1], 1), HIST // 8, HIST).astype(jnp.int32)
    new_slot = draw_new_slot(jax.random.fold_in(key_list[9], 71), 0)
    unique_ids = draw_unique_ids(jax.random.fold_in(key_list[9], 71), 0)
    inverse = draw_inverse(jax.random.fold_in(key_list[9], 71), 0)
    table = noise(key_list[5], (ITEMS, D), 1.0, 6.0, ((0, 128),))
    w_qu = noise(key_list[6], (D, 2 * D), D ** -0.5, 0.25)
    w_out = noise(key_list[7], (D, D), D ** -0.5, 0.25)
    w_head = noise(key_list[8], (D,), D ** -0.5, 0.25)
    return dict(cache=cache, lengths=lengths, new_slot=new_slot, unique_ids=unique_ids, inverse=inverse, table=table, w_qu=w_qu, w_out=w_out, w_head=w_head)


def attend_block(queries, group, first, lens):
    rows, sessions, width = queries.shape
    span = group.shape[1]
    size = width // HEADS
    query_heads = queries.astype(jnp.float32).reshape(rows, sessions, HEADS, size)
    keys = group[:, :, 0, :].astype(jnp.float32).reshape(sessions, span, HEADS, size)
    values = group[:, :, 1, :].astype(jnp.float32).reshape(sessions, span, HEADS, size)
    logits = jnp.einsum('rshd,sehd->shre', query_heads, keys) * (1.0 / math.sqrt(size))
    position = first + jnp.arange(span, dtype=jnp.int32)
    live = position[None, :] < lens[:, None]
    weights = jnp.where(live[:, None, None, :], jax.nn.silu(logits), 0.0).astype(jnp.bfloat16)
    mixed = jnp.einsum('shre,sehd->rshd', weights.astype(jnp.float32), values)
    return mixed.reshape(rows, sessions, width)

def attend(queries, group, first, lens):
    rows, sessions, width = queries.shape
    span = group.shape[1]
    row_block = 512 if rows % 512 == 0 else rows
    key_block = 512 if span % 512 == 0 else span
    turns = span // key_block

    def one_rows(block):

        def step(total, index):
            piece = lax.dynamic_slice_in_dim(group, index * key_block, key_block, 1)
            return (total + attend_block(block, piece, first + index * key_block, lens), None)
        start = jnp.zeros((block.shape[0], sessions, width), jnp.float32)
        total, _ = lax.scan(step, start, jnp.arange(turns, dtype=jnp.int32))
        return total
    blocks = queries.reshape(rows // row_block, row_block, sessions, width)
    return lax.map(one_rows, blocks).reshape(rows, sessions, width)

def reference(cache, lengths, new_slot, unique_ids, inverse, table, w_qu, w_out, w_head):
    migrated = jnp.zeros_like(cache).at[new_slot].set(cache)
    new_lengths = jnp.zeros_like(lengths).at[new_slot].set(lengths)
    total = cache.shape[0]
    count = inverse.shape[1]
    slot = jnp.arange(total, dtype=jnp.int32)[:, None]
    column = jnp.arange(count, dtype=jnp.int32)[None, :]
    picked = unique_ids[slot // SESS, column // NCD * U + inverse]
    candidates = jnp.take(table, picked.reshape(-1), axis=0)
    projected = jnp.dot(candidates, w_qu, preferred_element_type=jnp.float32)
    queries = projected[:, :D].astype(jnp.bfloat16).reshape(total, count, 1, D)
    gate = jax.nn.silu(projected[:, D:])

    def one_session(packed):
        query_rows, history, live_count = packed
        return attend(query_rows, history[None], jnp.int32(0), live_count[None])
    mixed = lax.map(one_session, (queries, migrated, new_lengths)).reshape(total * count, D)
    normed = mixed * lax.rsqrt(lax.optimization_barrier(jnp.mean(mixed * mixed, axis=-1, keepdims=True)) + 1e-06)
    gated = (normed * gate).astype(jnp.bfloat16)
    hidden = candidates.astype(jnp.float32) + jnp.dot(gated, w_out, preferred_element_type=jnp.float32)
    scores = lax.optimization_barrier(jnp.sum(hidden * w_head.astype(jnp.float32)[None, :], axis=1)).reshape(total, count)
    return (migrated, scores)
```

```python
import functools
import math

import jax
import jax.numpy as jnp
from jax import lax
from jax.experimental import pallas as pl
from jax.experimental.pallas import tpu as pltpu
from jax.sharding import PartitionSpec as P

HEADS = 4
CHUNKS = 4
ZN = 4
XN = 4
QCAP = 4
BF = jnp.bfloat16
F32 = jnp.float32
I32 = jnp.int32


def iota(shape, dim):
    return lax.broadcasted_iota(I32, shape, dim)


def dot(a, b):
    return jnp.dot(a, b, preferred_element_type=F32)


def dot_nt(a, b):
    return lax.dot_general(a, b, (((1,), (1,)), ((), ())), preferred_element_type=F32)


def kernel(
    ns_ref, ln_ref, ids_ref, inv_ref, cache_ref, table_ref, wqu_ref, wout_ref, whead_ref,
    mig_out, score_out,
    table, sendbuf, inc0, inc1, inc2, inc3, migbuf, kv,
    meta_own, meta, ns_vec, ns_smem, len_vec,
    ids_pad, inv_pad, req_own, req1, req2, req3, col, acc, resp, back, turned, fetched,
    pick, csend, cand, query, gate, mixed, ssend, sback,
    table_sem, small_sem, out_sem,
    meta_s, meta_r, m_s, m_r, z_s, z_r, x_s, x_r, f_s, f_r,
    q1_s, q1_r, q2_s, q2_r, p1_s, p1_r, p2_s, p2_r, c_s, c_r, o_s, o_r,
):
    incoming = (inc0, inc1, inc2, inc3)
    sess = lax.axis_index("session")
    item = lax.axis_index("item")
    x = item // ZN
    z = item % ZN
    span = kv.shape[4]
    width = cache_ref.shape[3]
    size = width // HEADS
    count = inv_ref.shape[1]
    items = table.shape[0]

    def speer(d):
        return lax.rem(sess + d, 8)

    def ipeer(d):
        return lax.rem(item + d, 16)

    def zpeer(d):
        return lax.rem(z + d, ZN)

    def xpeer(d):
        return lax.rem(x + d, XN)

    def remote(src, dst, ssem, rsem, s_to, i_to):
        return pltpu.make_async_remote_copy(
            src_ref=src, dst_ref=dst, send_sem=ssem, recv_sem=rsem,
            device_id=(s_to, i_to), device_id_type=pl.DeviceIdType.MESH,
        )

    def each(low, high, body):
        def step(d, carry):
            body(d)
            return carry
        lax.fori_loop(low, high, step, 0)

    load_table = pltpu.make_async_copy(table_ref, table, table_sem)
    load_table.start()

    barrier = pltpu.get_barrier_semaphore()

    def greet_session(d):
        pl.semaphore_signal(barrier, inc=1, device_id=(speer(d), item), device_id_type=pl.DeviceIdType.MESH)

    def greet_item(d):
        pl.semaphore_signal(barrier, inc=1, device_id=(sess, ipeer(d)), device_id_type=pl.DeviceIdType.MESH)

    each(1, 8, greet_session)
    each(1, 16, greet_item)

    lanes = ids_pad.shape[1]
    ids_pad[...] = jnp.full(ids_pad.shape, -1, I32)
    ids_pad[0:1, 0:ids_ref.shape[1]] = ids_ref[...]
    ids = ids_pad[0:1, :]
    holder = lax.shift_right_arithmetic(ids, 13)
    row = (ids - holder * items).astype(F32)
    peer = iota((128, lanes), 0)
    member = peer == holder
    ones = jnp.where(member, 1.0, 0.0)
    lower = jnp.where(iota((lanes, lanes), 0) <= iota((lanes, lanes), 1), 1.0, 0.0)
    rank = dot(ones.astype(BF), lower.astype(BF)) * ones
    lane = iota((128, 128), 1)
    wanted = jnp.zeros((128, 128), F32)
    for q in range(QCAP):
        one = jnp.sum(jnp.where(rank == q + 1.0, row, 0.0), axis=1, keepdims=True)
        wanted = jnp.where(lane == q, one, wanted)
    req_own[...] = wanted.astype(I32)
    place = jnp.sum(jnp.where(member, (peer * QCAP).astype(F32) + rank - 1.0, 0.0), axis=0, keepdims=True)

    meta_lane = iota((8, 128), 1)
    meta_row = iota((8, 128), 0)
    mine = jnp.zeros((8, 128), I32)
    for j in range(4):
        both = jnp.where(meta_row == 0, ns_ref[j], ln_ref[j])
        mine = jnp.where(meta_lane == j, both, mine)
    mine = jnp.where(meta_lane < 4, mine, -1)
    meta_own[...] = mine
    meta[sess] = mine

    def fill(e, d):
        to = speer(d)
        which = jnp.int32(0)
        for j in range(4):
            which = jnp.where(lax.shift_right_arithmetic(ns_ref[j], 2) == to, j, which)
        return cache_ref[which, :, e * span:(e + 1) * span, :]

    def prepare(e):
        def body(d):
            sendbuf[e, d] = fill(e, d)
        incoming[e][sess] = fill(e, 0)
        each(1, 8, body)

    def migrate(e, d):
        return remote(sendbuf.at[e, d], incoming[e].at[sess], m_s.at[e, d], m_r.at[e, d], speer(d), item)

    def request_s(d):
        to = speer(d)
        return remote(
            req_own.at[pl.ds(pl.multiple_of(to * 16, 16), 16)],
            req1.at[pl.ds(pl.multiple_of(sess * 16, 16), 16)],
            q1_s.at[d], q1_r.at[d], to, item)

    def request_i(d):
        to = ipeer(d)
        return remote(req2.at[to], req3.at[item], q2_s.at[d], q2_r.at[d], sess, to)

    def response_i(d):
        to = ipeer(d)
        return remote(resp.at[to], back.at[item], p1_s.at[d], p1_r.at[d], sess, to)

    def response_s(d):
        to = speer(d)
        return remote(turned.at[to], fetched.at[sess], p2_s.at[d], p2_r.at[d], to, item)

    def tell(d):
        return remote(meta_own, meta.at[sess], meta_s.at[d], meta_r.at[d], speer(d), item)

    def gather_z(e, d):
        to = zpeer(d)
        return remote(migbuf.at[e, to], kv.at[e, 0, ZN - d], z_s.at[e, d], z_r.at[e, d], sess, x * ZN + to)

    def ring_x(e, way):
        to = xpeer(1 if way == 0 else 3)
        return remote(kv.at[e, 0], kv.at[e, 3 if way == 0 else 1], x_s.at[e, way], x_r.at[e, way], sess, to * ZN + z)

    def forward_x(e, way):
        to = xpeer(1 if way == 0 else 3)
        part = pl.ds(0, 2) if way == 0 else pl.ds(2, 2)
        return remote(
            kv.at[e, 3 if way == 0 else 1, part], kv.at[e, 2, part],
            f_s.at[e, way], f_r.at[e, way], sess, to * ZN + z)

    def send_cand(d):
        return remote(csend.at[d], cand.at[ZN - d], c_s.at[d], c_r.at[d], sess, x * ZN + zpeer(d))

    def send_score(d):
        return remote(ssend.at[d], sback.at[ZN - d], o_s.at[d], o_r.at[d], sess, x * ZN + zpeer(d))

    prepare(0)
    pl.semaphore_wait(barrier, 22)
    each(1, 8, lambda d: request_s(d).start())
    each(1, 8, lambda d: tell(d).start())
    each(1, 8, lambda d: migrate(0, d).start())
    prepare(1)
    each(1, 8, lambda d: migrate(1, d).start())
    own = pl.ds(pl.multiple_of(sess * 16, 16), 16)
    req1[own] = req_own[own]

    each(1, 8, lambda d: request_s(d).wait_recv())
    for i in range(16):
        req2[i] = req1[pl.ds(i, 8, stride=16), :]
    req3[item] = req2[item]
    each(1, 16, lambda d: request_i(d).start())

    put = jnp.where(iota((512, lanes), 0).astype(F32) == place, 1.0, 0.0).astype(BF)
    inv_pad[...] = jnp.zeros(inv_pad.shape, F32)
    inv_pad[0:4, :] = inv_ref[...].astype(F32)
    inv_col = jnp.transpose(inv_pad[...])
    for j in range(4):
        hot = jnp.where(iota((count, lanes), 1).astype(F32) == inv_col[:, j:j + 1], 1.0, 0.0).astype(BF)
        pick[j] = dot_nt(hot, put).astype(BF)

    prepare(2)
    each(1, 8, lambda d: migrate(2, d).start())
    prepare(3)
    each(1, 8, lambda d: migrate(3, d).start())

    each(1, 8, lambda d: tell(d).wait_recv())
    slots = jnp.zeros((8, 128), I32)
    live = jnp.zeros((1, 128), I32)
    for o in range(8):
        first = meta[o, 0:1, :]
        slots = jnp.where(meta_row == o, first, slots)
        live = live + jnp.where(first == sess * 4 + z, meta[o, 1:2, :], 0)
    live = jnp.sum(live.astype(F32), axis=1, keepdims=True)
    len_vec[...] = jnp.broadcast_to(live, (8, 128)).astype(I32)
    ns_vec[...] = slots
    to_smem = pltpu.make_async_copy(ns_vec, ns_smem, small_sem)
    to_smem.start()
    to_smem.wait()

    def source(k):
        src = jnp.int32(0)
        for o in range(8):
            for j in range(4):
                src = jnp.where(ns_smem[o, j] == sess * 4 + k, o, src)
        return src

    sources = [source(k) for k in range(4)]

    def store_out(e):
        return pltpu.make_async_copy(migbuf.at[e], mig_out.at[:, :, pl.ds(e * span, span), :], out_sem.at[e])

    def settle(e):
        each(1, 8, lambda d: migrate(e, d).wait_recv())
        for k in range(4):
            migbuf[e, k] = incoming[e][sources[k]]
        kv[e, 0, 0] = migbuf[e, z]
        each(1, ZN, lambda d: gather_z(e, d).start())
        store_out(e).start()

    def spread(e):
        each(1, ZN, lambda d: gather_z(e, d).wait_recv())
        for way in range(2):
            ring_x(e, way).start()

    def onward(e):
        for way in range(2):
            ring_x(e, way).wait_recv()
            forward_x(e, way).start()

    def arrive(e):
        for way in range(2):
            forward_x(e, way).wait_recv()

    each(1, 16, lambda d: request_i(d).wait_recv())
    for i in range(16):
        asked = req3[i]
        for q in range(QCAP):
            col[i * 32 + q * 8:i * 32 + q * 8 + 8, :] = jnp.broadcast_to(asked[:, q:q + 1], (8, 128))
    load_table.wait()
    acc[...] = jnp.zeros(acc.shape, F32)
    depth = 1024

    def look_up(c):
        base = c * depth
        want = col[...] - iota(col.shape, 1) - base
        hot = jnp.concatenate(
            [jnp.where(want == t * 128, 1.0, 0.0).astype(BF) for t in range(depth // 128)], axis=1)
        acc[...] += dot(hot, table[pl.ds(pl.multiple_of(base, depth), depth), :])

    each(0, items // depth, look_up)
    for i in range(16):
        resp[i] = acc[i * 32:(i + 1) * 32, :].astype(BF)
    back[item] = resp[item]
    each(1, 16, lambda d: response_i(d).start())

    settle(0)
    settle(1)
    spread(0)

    each(1, 16, lambda d: response_i(d).wait_recv())
    out_row = iota((512, 512), 0)
    in_row = lax.rem(out_row, 64) // 4 * 32 + lax.rem(out_row, 4) * 8 + out_row // 64
    turn = jnp.where(in_row == iota((512, 512), 1), 1.0, 0.0).astype(BF)
    turned[...] = dot(turn, back[...].reshape(512, width)).astype(BF).reshape(8, 64, width)
    fetched[sess] = turned[sess]
    each(1, 8, lambda d: response_s(d).start())

    spread(1)
    onward(0)
    settle(2)
    spread(2)
    onward(1)

    each(1, 8, lambda d: response_s(d).wait_recv())

    def make_cand(d):
        return dot(pick[zpeer(d)], fetched[...].reshape(512, width)).astype(BF)

    for d in range(1, ZN):
        csend[d] = make_cand(d)
        send_cand(d).start()
    cand[0] = make_cand(0)

    settle(3)
    spread(3)
    onward(2)

    def project(r):
        rows = cand[r]
        query[r] = dot(rows, wqu_ref[:, 0:width]).astype(BF)
        g = dot(rows, wqu_ref[:, width:])
        gate[r] = g / (1.0 + jnp.exp(-g))
        mixed[r] = jnp.zeros(mixed.shape[1:], F32)

    each(1, ZN, lambda d: send_cand(d).wait_recv())
    each(0, ZN, project)

    def attend(e):
        half = 0.5 / math.sqrt(size)
        spot = iota((1, ZN * span), 1)
        where = lax.rem(z + spot // span, ZN) * (ZN * 64) + lax.rem(spot, span) + e * span
        scales = []
        for s in range(XN):
            position = xpeer(s) * (ZN * 256) + where
            alive = position < jnp.broadcast_to(len_vec[0:1, 0:1], position.shape)
            scales.append(jnp.where(alive, half, 0.0))

        def rows(r):
            for h in range(HEADS):
                cols = slice(h * size, (h + 1) * size)
                q = query[r, :, cols]
                total = mixed[r, :, cols]
                for s in range(XN):
                    keys = kv[e, s, :, 0, :, cols].reshape(ZN * span, size)
                    values = kv[e, s, :, 1, :, cols].reshape(ZN * span, size)
                    u = dot_nt(q, keys) * scales[s]
                    w = (u + u * jnp.tanh(u)).astype(BF)
                    total = total + dot(w, values)
                mixed[r, :, cols] = total

        each(0, ZN, rows)

    arrive(0)
    attend(0)
    onward(3)
    arrive(1)
    attend(1)
    arrive(2)
    attend(2)
    arrive(3)
    attend(3)

    head = jnp.broadcast_to(whead_ref[...], (16, width))
    fold = dot_nt(head, wout_ref[...])
    fold0 = fold.astype(BF)
    left = fold - fold0.astype(F32)
    fold1 = left.astype(BF)
    fold2 = (left - fold1.astype(F32)).astype(BF)
    which_row = iota((16, width), 0)
    folds = jnp.where(
        which_row == 0, fold0.astype(F32),
        jnp.where(which_row == 1, fold1.astype(F32), jnp.where(which_row == 2, fold2.astype(F32), 0.0))).astype(BF)
    heads = jnp.where(which_row == 0, head.astype(F32), 0.0).astype(BF)

    def finish(r):
        m = mixed[r]
        normed = m * lax.rsqrt(jnp.mean(m * m, axis=1, keepdims=True) + 1e-6)
        gated = (normed * gate[r]).astype(BF)
        part = dot_nt(folds, gated) + dot_nt(heads, cand[r])
        line = jnp.sum(part, axis=0, keepdims=True)
        ssend[r] = jnp.broadcast_to(line, (8, count))

    def finish_send(d):
        finish(d)
        send_score(d).start()

    each(1, ZN, finish_send)
    finish(0)
    sback[0] = ssend[0]
    each(1, ZN, lambda d: send_score(d).wait_recv())
    for j in range(4):
        score_out[j:j + 1, :] = sback[lax.rem(j - z + ZN, ZN), 0:1, :]

    each(1, 8, lambda d: request_s(d).wait_send())
    each(1, 8, lambda d: tell(d).wait_send())
    each(1, 16, lambda d: request_i(d).wait_send())
    each(1, 16, lambda d: response_i(d).wait_send())
    each(1, 8, lambda d: response_s(d).wait_send())
    each(1, ZN, lambda d: send_cand(d).wait_send())
    each(1, ZN, lambda d: send_score(d).wait_send())
    for e in range(CHUNKS):
        each(1, 8, lambda d: migrate(e, d).wait_send())
        each(1, ZN, lambda d: gather_z(e, d).wait_send())
        for way in range(2):
            ring_x(e, way).wait_send()
            forward_x(e, way).wait_send()
        store_out(e).wait()


def per_device(cache, lengths, new_slot, unique_ids, inverse, table, w_qu, w_out, w_head):
    sessions, events, _, width = cache.shape
    span = events // CHUNKS
    count = inverse.shape[1]
    split = cache.transpose(0, 2, 1, 3)
    vm = pl.BlockSpec(memory_space=pltpu.VMEM)
    sm = pl.BlockSpec(memory_space=pltpu.SMEM)
    hb = pl.BlockSpec(memory_space=pl.ANY)
    dma = pltpu.SemaphoreType.DMA
    chunk = (2, span, width)
    scratch = [
        pltpu.VMEM(table.shape, BF),
        pltpu.VMEM((CHUNKS, 8) + chunk, BF),
        pltpu.VMEM((8,) + chunk, BF),
        pltpu.VMEM((8,) + chunk, BF),
        pltpu.VMEM((8,) + chunk, BF),
        pltpu.VMEM((8,) + chunk, BF),
        pltpu.VMEM((CHUNKS, 4) + chunk, BF),
        pltpu.VMEM((CHUNKS, XN, ZN) + chunk, BF),
        pltpu.VMEM((8, 128), I32),
        pltpu.VMEM((8, 8, 128), I32),
        pltpu.VMEM((8, 128), I32),
        pltpu.SMEM((8, 128), I32),
        pltpu.VMEM((8, 128), I32),
        pltpu.VMEM((8, 384), I32),
        pltpu.VMEM((8, count), F32),
        pltpu.VMEM((128, 128), I32),
        pltpu.VMEM((128, 128), I32),
        pltpu.VMEM((16, 8, 128), I32),
        pltpu.VMEM((16, 8, 128), I32),
        pltpu.VMEM((512, 128), I32),
        pltpu.VMEM((512, width), F32),
        pltpu.VMEM((16, 32, width), BF),
        pltpu.VMEM((16, 32, width), BF),
        pltpu.VMEM((8, 64, width), BF),
        pltpu.VMEM((8, 64, width), BF),
        pltpu.VMEM((4, count, 512), BF),
        pltpu.VMEM((4, count, width), BF),
        pltpu.VMEM((4, count, width), BF),
        pltpu.VMEM((4, count, width), BF),
        pltpu.VMEM((4, count, width), F32),
        pltpu.VMEM((4, count, width), F32),
        pltpu.VMEM((4, 8, count), F32),
        pltpu.VMEM((4, 8, count), F32),
        dma, dma, dma((CHUNKS,)),
        dma((8,)), dma((8,)),
        dma((CHUNKS, 8)), dma((CHUNKS, 8)),
        dma((CHUNKS, ZN)), dma((CHUNKS, ZN)),
        dma((CHUNKS, 2)), dma((CHUNKS, 2)),
        dma((CHUNKS, 2)), dma((CHUNKS, 2)),
        dma((8,)), dma((8,)), dma((16,)), dma((16,)),
        dma((16,)), dma((16,)), dma((8,)), dma((8,)),
        dma((ZN,)), dma((ZN,)), dma((ZN,)), dma((ZN,)),
    ]
    migrated, scores = pl.pallas_call(
        kernel,
        out_shape=(
            jax.ShapeDtypeStruct(split.shape, BF),
            jax.ShapeDtypeStruct((sessions, count), F32),
        ),
        in_specs=[sm, sm, vm, vm, vm, hb, vm, vm, vm],
        out_specs=(hb, vm),
        scratch_shapes=scratch,
        compiler_params=pltpu.CompilerParams(
            collective_id=0, has_side_effects=True, vmem_limit_bytes=56 * 1024 * 1024),
        cost_estimate=pl.CostEstimate(flops=12_000_000_000, bytes_accessed=16_000_000, transcendentals=17_000_000),
    )(new_slot, lengths, unique_ids, inverse, split, table, w_qu, w_out, w_head.reshape(1, width))
    return migrated.transpose(0, 2, 1, 3), scores


def solution(mesh):
    placed = (
        P("session", "item", None, None),
        P("session"),
        P("session"),
        P("session", "item"),
        P("session", "item"),
        P(("session", "item"), None),
        P(),
        P(),
        P(),
    )
    return jax.shard_map(
        per_device,
        mesh=mesh,
        in_specs=placed,
        out_specs=(P("session", "item", None, None), P("session", "item")),
        check_vma=False,
    )
```

```python
import functools
import math

import jax
import jax.numpy as jnp
from jax import lax
from jax.experimental import pallas as pl
from jax.experimental.pallas import tpu as pltpu
from jax.sharding import PartitionSpec as P

HEADS = 4
CHUNKS = 8
AHEAD = 2
ZN = 4
XN = 4
QCAP = 4
BF = jnp.bfloat16
F32 = jnp.float32
I32 = jnp.int32


def iota(shape, dim):
    return lax.broadcasted_iota(I32, shape, dim)


def dot(a, b):
    return jnp.dot(a, b, preferred_element_type=F32)


def dot_nt(a, b):
    return lax.dot_general(a, b, (((1,), (1,)), ((), ())), preferred_element_type=F32)


def kernel(
    ns_ref, ln_ref, ids_ref, inv_ref, cache_hbm, table_ref, wqu_hbm, wout_hbm, whead_ref,
    mig_out, score_out,
    cache_ref, wqu_ref, wout_ref, table, sendbuf, inc0, inc1, inc2, inc3, inc4, inc5, inc6, inc7, migbuf, split, parted, kv,
    meta_own, meta, ns_vec, ns_smem, len_vec,
    ids_pad, inv_pad, req_own, req1, req2, req3, col, acc, resp, back, turned, fetched,
    turn, pick, csend, cand, query, gate, mixed, ssend, sback,
    cache_sem, wqu_sem, wout_sem, table_sem, small_sem, out_sem,
    meta_s, meta_r, m_s, m_r, z_s, z_r, x_s, x_r, f_s, f_r,
    q1_s, q1_r, q2_s, q2_r, p1_s, p1_r, p2_s, p2_r, c_s, c_r, o_s, o_r,
):
    incoming = (inc0, inc1, inc2, inc3, inc4, inc5, inc6, inc7)
    sess = lax.axis_index("session")
    item = lax.axis_index("item")
    x = item // ZN
    z = item % ZN
    span = kv.shape[4]
    block = 2 * HEADS * span
    width = wout_ref.shape[0]
    size = width // HEADS
    count = inv_ref.shape[1]
    items = table.shape[0]

    def speer(d):
        return lax.rem(sess + d, 8)

    def ipeer(d):
        return lax.rem(item + d, 16)

    core = lax.rem(sess, 2)
    sx = lax.rem(x + XN - core, XN)
    sz = lax.rem(z + ZN - core, ZN)
    px = sx + 1 - 2 * lax.rem(sx, 2)
    pz = sz + 1 - 2 * lax.rem(sz, 2)

    def device(ax, az):
        return lax.rem(ax + core, XN) * ZN + lax.rem(az + core, ZN)

    def mirror(g):
        return sx + g // 2 * (3 - 2 * sx), sz + g % 2 * (3 - 2 * sz)

    def square(ax, az):
        return ax // 2 * 2 + az // 2

    def session_of(g):
        return square(*mirror(g))

    def remote(src, dst, ssem, rsem, s_to, i_to):
        return pltpu.make_async_remote_copy(
            src_ref=src, dst_ref=dst, send_sem=ssem, recv_sem=rsem,
            device_id=(s_to, i_to), device_id_type=pl.DeviceIdType.MESH,
        )

    def each(low, high, body):
        def step(d, carry):
            body(d)
            return carry
        lax.fori_loop(low, high, step, 0)

    def wait_bytes(ref, sem):
        pltpu.make_async_copy(ref, ref, sem).wait()

    load_cache = pltpu.make_async_copy(cache_hbm, cache_ref, cache_sem)
    load_cache.start()
    load_table = pltpu.make_async_copy(table_ref, table, table_sem)
    load_table.start()
    load_wqu = pltpu.make_async_copy(wqu_hbm, wqu_ref, wqu_sem)
    load_wqu.start()
    load_wout = pltpu.make_async_copy(wout_hbm, wout_ref, wout_sem)
    load_wout.start()

    barrier = pltpu.get_barrier_semaphore()

    def greet_session(d):
        pl.semaphore_signal(barrier, inc=1, device_id=(speer(d), item), device_id_type=pl.DeviceIdType.MESH)

    def greet_item(d):
        pl.semaphore_signal(barrier, inc=1, device_id=(sess, ipeer(d)), device_id_type=pl.DeviceIdType.MESH)

    each(1, 8, greet_session)
    each(1, 16, greet_item)

    lanes = ids_pad.shape[1]
    ids_pad[...] = jnp.full(ids_pad.shape, -1, I32)
    ids_pad[0:1, 0:ids_ref.shape[1]] = ids_ref[...]
    ids = ids_pad[0:1, :]
    holder = lax.shift_right_arithmetic(ids, 13)
    row = (ids - holder * items).astype(F32)
    peer = iota((128, lanes), 0)
    member = peer == holder
    ones = jnp.where(member, 1.0, 0.0)
    lower = jnp.where(iota((lanes, lanes), 0) <= iota((lanes, lanes), 1), 1.0, 0.0)
    rank = dot(ones.astype(BF), lower.astype(BF)) * ones
    lane = iota((128, 128), 1)
    wanted = jnp.zeros((128, 128), F32)
    for q in range(QCAP):
        one = jnp.sum(jnp.where(rank == q + 1.0, row, 0.0), axis=1, keepdims=True)
        wanted = jnp.where(lane == q, one, wanted)
    req_own[...] = wanted.astype(I32)
    place = jnp.sum(jnp.where(member, (peer * QCAP).astype(F32) + rank - 1.0, 0.0), axis=0, keepdims=True)

    meta_lane = iota((8, 128), 1)
    meta_row = iota((8, 128), 0)
    mine = jnp.zeros((8, 128), I32)
    for j in range(4):
        both = jnp.where(meta_row == 0, ns_ref[j], ln_ref[j])
        mine = jnp.where(meta_lane == j, both, mine)
    mine = jnp.where(meta_lane < 4, mine, -1)
    meta_own[...] = mine
    meta[sess] = mine

    def fill(e, d):
        to = speer(d)
        which = jnp.int32(0)
        for j in range(4):
            which = jnp.where(lax.shift_right_arithmetic(ns_ref[j], 2) == to, j, which)
        return cache_ref[which, e * block:(e + 1) * block, :]

    def prepare(e):
        def body(d):
            sendbuf[e, d] = fill(e, d)
        incoming[e][sess] = fill(e, 0)
        each(1, 8, body)

    def migrate(e, d):
        return remote(sendbuf.at[e, d], incoming[e].at[sess], m_s, m_r.at[e], speer(d), item)

    def request_s(d):
        to = speer(d)
        return remote(
            req_own.at[pl.ds(pl.multiple_of(to * 16, 16), 16)],
            req1.at[pl.ds(pl.multiple_of(sess * 16, 16), 16)],
            q1_s, q1_r, to, item)

    def request_i(d):
        to = ipeer(d)
        return remote(req2.at[to], req3.at[item], q2_s, q2_r, sess, to)

    def response_i(d):
        to = ipeer(d)
        return remote(resp.at[to], back.at[item], p1_s, p1_r, sess, to)

    def response_s(d):
        to = speer(d)
        return remote(turned.at[to], fetched.at[sess], p2_s, p2_r, to, item)

    def tell(d):
        return remote(meta_own, meta.at[sess], meta_s, meta_r, speer(d), item)

    def enter(e, g):
        return remote(
            parted.at[e, session_of(g)], kv.at[e, 0, g], z_s, z_r.at[e], sess, device(*mirror(g)))

    def pair(e, way):
        to = device(px, sz) if way == 0 else device(sx, pz)
        return remote(kv.at[e, 0], kv.at[e, 2 if way == 0 else 1], x_s, x_r.at[e], sess, to)

    def across(e, way):
        to = device(sx, pz) if way == 0 else device(px, sz)
        part = pl.ds(0, 2) if way == 0 else pl.ds(2, 2)
        return remote(
            kv.at[e, 2 if way == 0 else 1, part], kv.at[e, 3, part], f_s, f_r.at[e], sess, to)

    def send_cand(g):
        return remote(csend.at[g], cand.at[g], c_s, c_r, sess, device(*mirror(g)))

    def send_score(g):
        return remote(ssend.at[g], sback.at[g], o_s, o_r, sess, device(*mirror(g)))

    def settle(e):
        wait_bytes(incoming[e].at[pl.ds(0, 7)], m_r.at[e])
        if e + AHEAD < CHUNKS:
            prepare(e + AHEAD)
            each(1, 8, lambda d: migrate(e + AHEAD, d).start())
        for k in range(4):
            rows = incoming[e][sources[k]]
            migbuf[e, k] = rows
            parted[e, k] = dot(split[...], rows).astype(BF).reshape(2 * HEADS, span, size)
        each(1, 4, lambda g: enter(e, g).start())
        kv[e, 0, 0] = parted[e, session_of(0)]
        store_out(e).start()

    def spread(e):
        wait_bytes(kv.at[e, 0, pl.ds(0, 3)], z_r.at[e])
        for way in range(2):
            pair(e, way).start()

    def onward(e):
        wait_bytes(kv.at[e, pl.ds(1, 2)], x_r.at[e])
        for way in range(2):
            across(e, way).start()

    def arrive(e):
        wait_bytes(kv.at[e, 3], f_r.at[e])

    def store_out(e):
        return pltpu.make_async_copy(migbuf.at[e], mig_out.at[:, pl.ds(e * block, block), :], out_sem)

    load_cache.wait()
    for e in range(AHEAD):
        prepare(e)
    pl.semaphore_wait(barrier, 22)
    each(1, 8, lambda d: request_s(d).start())
    each(1, 8, lambda d: tell(d).start())
    for e in range(AHEAD):
        each(1, 8, functools.partial(lambda e, d: migrate(e, d).start(), e))
    own = pl.ds(pl.multiple_of(sess * 16, 16), 16)
    req1[own] = req_own[own]

    to_row = iota((block, block), 0)
    from_row = lax.rem(to_row, span) * (2 * HEADS) + to_row // span
    split[...] = jnp.where(from_row == iota((block, block), 1), 1.0, 0.0).astype(BF)
    put = jnp.where(iota((512, lanes), 0).astype(F32) == place, 1.0, 0.0).astype(BF)
    inv_pad[...] = jnp.zeros(inv_pad.shape, F32)
    inv_pad[0:4, :] = inv_ref[...].astype(F32)
    inv_col = jnp.transpose(inv_pad[...])
    for j in range(4):
        hot = jnp.where(iota((count, lanes), 1).astype(F32) == inv_col[:, j:j + 1], 1.0, 0.0).astype(BF)
        pick[j] = dot_nt(hot, put).astype(BF)
    out_row = iota((512, 512), 0)
    in_row = lax.rem(out_row, 64) // 4 * 32 + lax.rem(out_row, 4) * 8 + out_row // 64
    turn[...] = jnp.where(in_row == iota((512, 512), 1), 1.0, 0.0).astype(BF)

    wait_bytes(req1.at[pl.ds(0, 112)], q1_r)
    for i in range(16):
        req2[i] = req1[pl.ds(i, 8, stride=16), :]
    req3[item] = req2[item]
    each(1, 16, lambda d: request_i(d).start())

    wait_bytes(meta.at[pl.ds(0, 7)], meta_r)
    slots = jnp.zeros((8, 128), I32)
    live = jnp.zeros((1, 128), I32)
    for o in range(8):
        first = meta[o, 0:1, :]
        slots = jnp.where(meta_row == o, first, slots)
        live = live + jnp.where(first == sess * 4 + session_of(0), meta[o, 1:2, :], 0)
    live = jnp.sum(live.astype(F32), axis=1, keepdims=True)
    len_vec[...] = jnp.broadcast_to(live, (8, 128)).astype(I32)
    ns_vec[...] = slots
    to_smem = pltpu.make_async_copy(ns_vec, ns_smem, small_sem)
    to_smem.start()
    to_smem.wait()

    def source(k):
        src = jnp.int32(0)
        for o in range(8):
            for j in range(4):
                src = jnp.where(ns_smem[o, j] == sess * 4 + k, o, src)
        return src

    sources = [source(k) for k in range(4)]

    settle(0)
    settle(1)

    wait_bytes(req3.at[pl.ds(0, 15)], q2_r)
    for i in range(16):
        asked = req3[i]
        for q in range(QCAP):
            col[i * 32 + q * 8:i * 32 + q * 8 + 8, :] = jnp.broadcast_to(asked[:, q:q + 1], (8, 128))
    load_table.wait()
    acc[...] = jnp.zeros(acc.shape, F32)
    depth = 1024

    def look_up(c):
        base = c * depth
        want = col[...] - iota(col.shape, 1) - base
        hot = jnp.concatenate(
            [jnp.where(want == t * 128, 1.0, 0.0).astype(BF) for t in range(depth // 128)], axis=1)
        acc[...] += dot(hot, table[pl.ds(pl.multiple_of(base, depth), depth), :])

    def look_ups(c):
        @pl.when(c == items // depth // 2)
        def _():
            spread(0)
            spread(1)

        look_up(c)

    each(0, items // depth, look_ups)
    for i in range(16):
        resp[i] = acc[i * 32:(i + 1) * 32, :].astype(BF)
    back[item] = resp[item]
    each(1, 16, lambda d: response_i(d).start())

    settle(2)
    onward(0)
    settle(3)
    onward(1)
    spread(2)

    wait_bytes(back.at[pl.ds(0, 15)], p1_r)
    turned[...] = dot(turn[...], back[...].reshape(512, width)).astype(BF).reshape(8, 64, width)
    fetched[sess] = turned[sess]
    each(1, 8, lambda d: response_s(d).start())

    settle(4)
    spread(3)
    onward(2)
    settle(5)
    spread(4)
    onward(3)

    wait_bytes(fetched.at[pl.ds(0, 7)], p2_r)

    def make_cand(g):
        return dot(pick[session_of(g)], fetched[...].reshape(512, width)).astype(BF)

    for g in range(1, 4):
        csend[g] = make_cand(g)
        send_cand(g).start()
    cand[0] = make_cand(0)

    settle(6)
    spread(5)
    onward(4)
    settle(7)
    spread(6)
    onward(5)

    load_wqu.wait()

    def project(r):
        rows = cand[r]
        query[r] = dot(rows, wqu_ref[:, 0:width]).astype(BF)
        g = dot(rows, wqu_ref[:, width:])
        gate[r] = g / (1.0 + jnp.exp(-g))
        mixed[r] = jnp.zeros(mixed.shape[1:], F32)

    wait_bytes(cand.at[pl.ds(1, 3)], c_r)
    each(0, 4, project)

    def attend(p):
        e = 2 * p

        @pl.when(p == 1)
        def _():
            spread(7)
            onward(6)

        @pl.when(p == 2)
        def _():
            onward(7)

        arrive(e)
        arrive(e + 1)
        half = 0.5 / math.sqrt(size)
        spot = iota((1, 8 * span), 1)
        group = lax.rem(spot, 4 * span) // span
        event = (e + spot // (4 * span)) * span + lax.rem(spot, span)
        scales = []
        for m in range(4):
            ax, az = (px if m // 2 else sx), (pz if m % 2 else sz)
            gx = ax + group // 2 * (3 - 2 * ax)
            gz = az + lax.rem(group, 2) * (3 - 2 * az)
            position = device(gx, gz) * (CHUNKS * span) + event
            alive = position < jnp.broadcast_to(len_vec[0:1, 0:1], position.shape)
            scales.append(jnp.where(alive, half, 0.0))

        def rows(r):
            for h in range(HEADS):
                cols = slice(h * size, (h + 1) * size)
                q = query[r, :, cols]
                total = mixed[r, :, cols]
                for m in range(4):
                    keys = kv[pl.ds(e, 2), m, :, 2 * h].reshape(8 * span, size)
                    values = kv[pl.ds(e, 2), m, :, 2 * h + 1].reshape(8 * span, size)
                    u = dot_nt(q, keys) * scales[m]
                    w = (u + u * jnp.tanh(u)).astype(BF)
                    total = total + dot(w, values)
                mixed[r, :, cols] = total

        each(0, 4, rows)

    each(0, CHUNKS // 2, attend)

    load_wout.wait()
    head = jnp.broadcast_to(whead_ref[...].astype(F32).reshape(1, width), (16, width)).astype(BF)
    fold = dot_nt(head, wout_ref[...])
    fold0 = fold.astype(BF)
    left = fold - fold0.astype(F32)
    fold1 = left.astype(BF)
    fold2 = (left - fold1.astype(F32)).astype(BF)
    which_row = iota((16, width), 0)
    folds = jnp.where(
        which_row == 0, fold0.astype(F32),
        jnp.where(which_row == 1, fold1.astype(F32), jnp.where(which_row == 2, fold2.astype(F32), 0.0))).astype(BF)
    heads = jnp.where(which_row == 0, head.astype(F32), 0.0).astype(BF)

    def finish(r):
        m = mixed[r]
        normed = m * lax.rsqrt(jnp.mean(m * m, axis=1, keepdims=True) + 1e-6)
        gated = (normed * gate[r]).astype(BF)
        part = dot_nt(folds, gated) + dot_nt(heads, cand[r])
        line = jnp.sum(part, axis=0, keepdims=True)
        ssend[r] = jnp.broadcast_to(line, (8, count))

    def finish_send(g):
        finish(g)
        send_score(g).start()

    each(1, 4, finish_send)
    finish(0)
    sback[0] = ssend[0]

    wait_bytes(req_own.at[pl.ds(0, 112)], q1_s)
    wait_bytes(meta.at[pl.ds(0, 7)], meta_s)
    wait_bytes(req2.at[pl.ds(0, 15)], q2_s)
    wait_bytes(resp.at[pl.ds(0, 15)], p1_s)
    wait_bytes(turned.at[pl.ds(0, 7)], p2_s)
    wait_bytes(csend.at[pl.ds(1, 3)], c_s)
    wait_bytes(sendbuf.at[:, pl.ds(1, 7)], m_s)
    wait_bytes(parted.at[:, pl.ds(0, 3)], z_s)
    wait_bytes(kv.at[:, pl.ds(1, 2)], x_s)
    wait_bytes(kv.at[:, 3], f_s)
    wait_bytes(migbuf, out_sem)
    wait_bytes(ssend.at[pl.ds(1, 3)], o_s)

    wait_bytes(sback.at[pl.ds(1, 3)], o_r)
    for j in range(4):
        line = jnp.zeros((1, count), F32)
        for g in range(4):
            line = jnp.where(session_of(g) == j, sback[g, 0:1, :], line)
        score_out[j:j + 1, :] = line


def hand_on(mig_ref, score_ref, mig_out, score_out, held, in_sem, out_sem):
    parts = 4
    span = mig_ref.shape[1] // parts
    pieces = [(k, pl.ds(t * span, span)) for k in range(mig_ref.shape[0]) for t in range(parts)]
    loads = [
        pltpu.make_async_copy(mig_ref.at[k, part], held.at[k, part], in_sem.at[n])
        for n, (k, part) in enumerate(pieces)]
    stores = [
        pltpu.make_async_copy(held.at[k, part], mig_out.at[k, part], out_sem.at[n])
        for n, (k, part) in enumerate(pieces)]
    for load in loads:
        load.start()
    score_out[...] = score_ref[...]
    for load, store in zip(loads, stores):
        load.wait()
        store.start()
    for store in stores:
        store.wait()


def per_device(cache, lengths, new_slot, unique_ids, inverse, table, w_qu, w_out, w_head):
    sessions, events, _, width = cache.shape
    span = events // CHUNKS
    count = inverse.shape[1]
    size = width // HEADS
    block = 2 * HEADS * span
    whole = cache.reshape(sessions, events, 2, HEADS, size).transpose(0, 1, 3, 2, 4)
    whole = whole.reshape(sessions, events * HEADS * 2, size)
    vm = pl.BlockSpec(memory_space=pltpu.VMEM)
    sm = pl.BlockSpec(memory_space=pltpu.SMEM)
    hb = pl.BlockSpec(memory_space=pl.ANY)
    dma = pltpu.SemaphoreType.DMA
    chunk = (block, size)
    scratch = [
        pltpu.VMEM(whole.shape, BF),
        pltpu.VMEM(w_qu.shape, BF),
        pltpu.VMEM(w_out.shape, BF),
        pltpu.VMEM(table.shape, BF),
        pltpu.VMEM((CHUNKS, 8) + chunk, BF),
        *[pltpu.VMEM((8,) + chunk, BF) for _ in range(CHUNKS)],
        pltpu.VMEM((CHUNKS, 4) + chunk, BF),
        pltpu.VMEM((block, block), BF),
        pltpu.VMEM((CHUNKS, 4, 2 * HEADS, span, size), BF),
        pltpu.VMEM((CHUNKS, 4, 4, 2 * HEADS, span, size), BF),
        pltpu.VMEM((8, 128), I32),
        pltpu.VMEM((8, 8, 128), I32),
        pltpu.VMEM((8, 128), I32),
        pltpu.SMEM((8, 128), I32),
        pltpu.VMEM((8, 128), I32),
        pltpu.VMEM((8, 384), I32),
        pltpu.VMEM((8, count), F32),
        pltpu.VMEM((128, 128), I32),
        pltpu.VMEM((128, 128), I32),
        pltpu.VMEM((16, 8, 128), I32),
        pltpu.VMEM((16, 8, 128), I32),
        pltpu.VMEM((512, 128), I32),
        pltpu.VMEM((512, width), F32),
        pltpu.VMEM((16, 32, width), BF),
        pltpu.VMEM((16, 32, width), BF),
        pltpu.VMEM((8, 64, width), BF),
        pltpu.VMEM((8, 64, width), BF),
        pltpu.VMEM((512, 512), BF),
        pltpu.VMEM((4, count, 512), BF),
        pltpu.VMEM((4, count, width), BF),
        pltpu.VMEM((4, count, width), BF),
        pltpu.VMEM((4, count, width), BF),
        pltpu.VMEM((4, count, width), F32),
        pltpu.VMEM((4, count, width), F32),
        pltpu.VMEM((4, 8, count), F32),
        pltpu.VMEM((4, 8, count), F32),
        dma, dma, dma, dma, dma, dma,
        dma, dma,
        dma, dma((CHUNKS,)),
        dma, dma((CHUNKS,)),
        dma, dma((CHUNKS,)),
        dma, dma((CHUNKS,)),
        dma, dma, dma, dma,
        dma, dma, dma, dma,
        dma, dma, dma, dma,
    ]
    migrated, scores = pl.pallas_call(
        kernel,
        out_shape=(
            jax.ShapeDtypeStruct(whole.shape, BF),
            jax.ShapeDtypeStruct((sessions, count), F32),
        ),
        in_specs=[sm, sm, vm, vm, hb, hb, hb, hb, vm],
        out_specs=(hb, vm),
        scratch_shapes=scratch,
        compiler_params=pltpu.CompilerParams(
            collective_id=0, has_side_effects=True, vmem_limit_bytes=56 * 1024 * 1024),
        cost_estimate=pl.CostEstimate(flops=12_000_000_000, bytes_accessed=16_000_000, transcendentals=17_000_000),
    )(new_slot, lengths, unique_ids, inverse, whole, table, w_qu, w_out, w_head)
    migrated, scores = pl.pallas_call(
        hand_on,
        out_shape=(
            jax.ShapeDtypeStruct(whole.shape, BF),
            jax.ShapeDtypeStruct((sessions, count), F32),
        ),
        in_specs=[hb, vm],
        out_specs=(hb, vm),
        scratch_shapes=[pltpu.VMEM(whole.shape, BF), dma((16,)), dma((16,))],
    )(migrated, scores)
    migrated = migrated.reshape(sessions, events, HEADS, 2, size).transpose(0, 1, 3, 2, 4)
    return migrated.reshape(cache.shape), scores


def solution(mesh):
    placed = (
        P("session", "item", None, None),
        P("session"),
        P("session"),
        P("session", "item"),
        P("session", "item"),
        P(("session", "item"), None),
        P(),
        P(),
        P(),
    )
    return jax.shard_map(
        per_device,
        mesh=mesh,
        in_specs=placed,
        out_specs=(P("session", "item", None, None), P("session", "item")),
        check_vma=False,
    )
```

```python
import functools
import math

import jax
import jax.numpy as jnp
from jax import lax
from jax.experimental import pallas as pl
from jax.experimental.pallas import tpu as pltpu
from jax.sharding import PartitionSpec as P

HEADS = 4
CHUNKS = 8
AHEAD = 2
ZN = 4
XN = 4
QCAP = 4
START = ("s0", "m2", "s1", "m3")
LOOK = {2: ("x0",), 5: ("x1", "s2", "m4")}
MIDDLE = ("o0", "s3", "m5", "x2", "o1")
LATER = ("s4", "m6", "x3", "o2", "s5", "m7", "x4", "o3")
LAST = ("s6", "x5", "o4")
LOOP = {(0, 0): ("s7", "x6", "o5"), (1, 0): ("x7", "o6"), (2, 0): ("o7",)}
BF = jnp.bfloat16
F32 = jnp.float32
I32 = jnp.int32


def iota(shape, dim):
    return lax.broadcasted_iota(I32, shape, dim)


def dot(a, b):
    return jnp.dot(a, b, preferred_element_type=F32)


def dot_nt(a, b):
    return lax.dot_general(a, b, (((1,), (1,)), ((), ())), preferred_element_type=F32)


def kernel(
    ns_ref, ln_ref, ids_ref, inv_ref, cache_hbm, table_ref, wqu_hbm, wout_hbm, whead_ref,
    mig_out, score_out,
    cache_ref, wqu_ref, wout_ref, table, sendbuf, inc0, inc1, inc2, inc3, inc4, inc5, inc6, inc7, migbuf, split, parted, kv,
    meta_own, meta, ns_vec, ns_smem, len_vec,
    ids_pad, inv_pad, req_own, req1, req2, req3, col, acc, resp, back, turned, fetched,
    turn, fold_ref, pick, csend, cand, query, gate, mixed, ssend, sback,
    cache_sem, wqu_sem, wout_sem, table_sem, small_sem, out_sem,
    meta_s, meta_r, m_s, m_r, z_s, z_r, x_s, x_r, f_s, f_r,
    q1_s, q1_r, q2_s, q2_r, p1_s, p1_r, p2_s, p2_r, c_s, c_r, o_s, o_r,
):
    incoming = (inc0, inc1, inc2, inc3, inc4, inc5, inc6, inc7)
    sess = lax.axis_index("session")
    item = lax.axis_index("item")
    x = item // ZN
    z = item % ZN
    span = kv.shape[4]
    block = 2 * HEADS * span
    width = wout_ref.shape[0]
    size = width // HEADS
    count = inv_ref.shape[1]
    items = table.shape[0]

    def speer(d):
        return lax.rem(sess + d, 8)

    def ipeer(d):
        return lax.rem(item + d, 16)

    core = lax.rem(sess, 2)
    sx = lax.rem(x + XN - core, XN)
    sz = lax.rem(z + ZN - core, ZN)
    px = sx + 1 - 2 * lax.rem(sx, 2)
    pz = sz + 1 - 2 * lax.rem(sz, 2)

    def device(ax, az):
        return lax.rem(ax + core, XN) * ZN + lax.rem(az + core, ZN)

    def mirror(g):
        return sx + g // 2 * (3 - 2 * sx), sz + g % 2 * (3 - 2 * sz)

    def square(ax, az):
        return ax // 2 * 2 + az // 2

    def session_of(g):
        return square(*mirror(g))

    def remote(src, dst, ssem, rsem, s_to, i_to):
        return pltpu.make_async_remote_copy(
            src_ref=src, dst_ref=dst, send_sem=ssem, recv_sem=rsem,
            device_id=(s_to, i_to), device_id_type=pl.DeviceIdType.MESH,
        )

    def each(low, high, body):
        def step(d, carry):
            body(d)
            return carry
        lax.fori_loop(low, high, step, 0)

    def wait_bytes(ref, sem):
        pltpu.make_async_copy(ref, ref, sem).wait()

    load_cache = pltpu.make_async_copy(cache_hbm, cache_ref, cache_sem)
    load_cache.start()
    load_table = pltpu.make_async_copy(table_ref, table, table_sem)
    load_table.start()
    load_wqu = pltpu.make_async_copy(wqu_hbm, wqu_ref, wqu_sem)
    load_wqu.start()
    load_wout = pltpu.make_async_copy(wout_hbm, wout_ref, wout_sem)
    load_wout.start()

    barrier = pltpu.get_barrier_semaphore()

    def greet_session(d):
        pl.semaphore_signal(barrier, inc=1, device_id=(speer(d), item), device_id_type=pl.DeviceIdType.MESH)

    def greet_item(d):
        pl.semaphore_signal(barrier, inc=1, device_id=(sess, ipeer(d)), device_id_type=pl.DeviceIdType.MESH)

    each(1, 8, greet_session)
    each(1, 16, greet_item)

    lanes = ids_pad.shape[1]
    ids_pad[...] = jnp.full(ids_pad.shape, -1, I32)
    ids_pad[0:1, 0:ids_ref.shape[1]] = ids_ref[...]
    ids = ids_pad[0:1, :]
    holder = lax.shift_right_arithmetic(ids, 13)
    row = (ids - holder * items).astype(F32)
    peer = iota((128, lanes), 0)
    member = peer == holder
    ones = jnp.where(member, 1.0, 0.0)
    lower = jnp.where(iota((lanes, lanes), 0) <= iota((lanes, lanes), 1), 1.0, 0.0)
    rank = dot(ones.astype(BF), lower.astype(BF)) * ones
    lane = iota((128, 128), 1)
    wanted = jnp.zeros((128, 128), F32)
    for q in range(QCAP):
        one = jnp.sum(jnp.where(rank == q + 1.0, row, 0.0), axis=1, keepdims=True)
        wanted = jnp.where(lane == q, one, wanted)
    req_own[...] = wanted.astype(I32)
    place = jnp.sum(jnp.where(member, (peer * QCAP).astype(F32) + rank - 1.0, 0.0), axis=0, keepdims=True)

    meta_lane = iota((8, 128), 1)
    meta_row = iota((8, 128), 0)
    mine = jnp.zeros((8, 128), I32)
    for j in range(4):
        both = jnp.where(meta_row == 0, ns_ref[j], ln_ref[j])
        mine = jnp.where(meta_lane == j, both, mine)
    mine = jnp.where(meta_lane < 4, mine, -1)
    meta_own[...] = mine
    meta[sess] = mine

    def fill(e, d):
        to = speer(d)
        which = jnp.int32(0)
        for j in range(4):
            which = jnp.where(lax.shift_right_arithmetic(ns_ref[j], 2) == to, j, which)
        return cache_ref[which, e * block:(e + 1) * block, :]

    def prepare(e):
        def body(d):
            sendbuf[e, d] = fill(e, d)
        incoming[e][sess] = fill(e, 0)
        each(1, 8, body)

    def migrate(e, d):
        return remote(sendbuf.at[e, d], incoming[e].at[sess], m_s, m_r.at[e], speer(d), item)

    def request_s(d):
        to = speer(d)
        return remote(
            req_own.at[pl.ds(pl.multiple_of(to * 16, 16), 16)],
            req1.at[pl.ds(pl.multiple_of(sess * 16, 16), 16)],
            q1_s, q1_r, to, item)

    def request_i(d):
        to = ipeer(d)
        return remote(req2.at[to], req3.at[item], q2_s, q2_r, sess, to)

    def response_i(d):
        to = ipeer(d)
        return remote(resp.at[to], back.at[item], p1_s, p1_r, sess, to)

    def response_s(d):
        to = speer(d)
        return remote(turned.at[to], fetched.at[sess], p2_s, p2_r, to, item)

    def tell(d):
        return remote(meta_own, meta.at[sess], meta_s, meta_r, speer(d), item)

    def enter(e, g):
        return remote(
            parted.at[e, session_of(g)], kv.at[e, 0, g], z_s, z_r.at[e], sess, device(*mirror(g)))

    def pair(e, way):
        to = device(px, sz) if way == 0 else device(sx, pz)
        return remote(kv.at[e, 0], kv.at[e, 2 if way == 0 else 1], x_s, x_r.at[e], sess, to)

    def across(e, way):
        to = device(sx, pz) if way == 0 else device(px, sz)
        part = pl.ds(0, 2) if way == 0 else pl.ds(2, 2)
        return remote(
            kv.at[e, 2 if way == 0 else 1, part], kv.at[e, 3, part], f_s, f_r.at[e], sess, to)

    def send_cand(g):
        return remote(csend.at[g], cand.at[g], c_s, c_r, sess, device(*mirror(g)))

    def send_score(g):
        return remote(ssend.at[g], sback.at[g], o_s, o_r, sess, device(*mirror(g)))

    def settle(e):
        wait_bytes(incoming[e].at[pl.ds(0, 7)], m_r.at[e])
        for k in range(4):
            rows = incoming[e][sources[k]]
            migbuf[e, k] = rows
            parted[e, k] = dot(split[...], rows).astype(BF).reshape(2 * HEADS, span, size)
        each(1, 4, lambda g: enter(e, g).start())
        kv[e, 0, 0] = parted[e, session_of(0)]
        store_out(e).start()

    def spread(e):
        wait_bytes(kv.at[e, 0, pl.ds(0, 3)], z_r.at[e])
        for way in range(2):
            pair(e, way).start()

    def onward(e):
        wait_bytes(kv.at[e, pl.ds(1, 2)], x_r.at[e])
        for way in range(2):
            across(e, way).start()

    def arrive(e):
        wait_bytes(kv.at[e, 3], f_r.at[e])

    def store_out(e):
        return pltpu.make_async_copy(migbuf.at[e], mig_out.at[:, pl.ds(e * block, block), :], out_sem)

    def launch(e):
        if e >= AHEAD:
            prepare(e)
        each(1, 8, lambda d: migrate(e, d).start())

    def steps(names):
        for name in names:
            {"m": launch, "s": settle, "x": spread, "o": onward}[name[0]](int(name[1:]))

    load_cache.wait()
    for e in range(AHEAD):
        prepare(e)
    pl.semaphore_wait(barrier, 22)
    each(1, 8, lambda d: request_s(d).start())
    each(1, 8, lambda d: tell(d).start())
    for e in range(AHEAD):
        launch(e)
    own = pl.ds(pl.multiple_of(sess * 16, 16), 16)
    req1[own] = req_own[own]

    to_row = iota((block, block), 0)
    from_row = lax.rem(to_row, span) * (2 * HEADS) + to_row // span
    split[...] = jnp.where(from_row == iota((block, block), 1), 1.0, 0.0).astype(BF)
    put = jnp.where(iota((512, lanes), 0).astype(F32) == place, 1.0, 0.0).astype(BF)
    inv_pad[...] = jnp.zeros(inv_pad.shape, F32)
    inv_pad[0:4, :] = inv_ref[...].astype(F32)
    inv_col = jnp.transpose(inv_pad[...])
    for j in range(4):
        hot = jnp.where(iota((count, lanes), 1).astype(F32) == inv_col[:, j:j + 1], 1.0, 0.0).astype(BF)
        pick[j] = dot_nt(hot, put).astype(BF)
    out_row = iota((512, 512), 0)
    in_row = lax.rem(out_row, 64) // 4 * 32 + lax.rem(out_row, 4) * 8 + out_row // 64
    turn[...] = jnp.where(in_row == iota((512, 512), 1), 1.0, 0.0).astype(BF)

    wait_bytes(req1.at[pl.ds(0, 112)], q1_r)
    for i in range(16):
        req2[i] = req1[pl.ds(i, 8, stride=16), :]
    req3[item] = req2[item]
    each(1, 16, lambda d: request_i(d).start())

    wait_bytes(meta.at[pl.ds(0, 7)], meta_r)
    slots = jnp.zeros((8, 128), I32)
    live = jnp.zeros((1, 128), I32)
    for o in range(8):
        first = meta[o, 0:1, :]
        slots = jnp.where(meta_row == o, first, slots)
        live = live + jnp.where(first == sess * 4 + session_of(0), meta[o, 1:2, :], 0)
    live = jnp.sum(live.astype(F32), axis=1, keepdims=True)
    len_vec[...] = jnp.broadcast_to(live, (8, 128)).astype(I32)
    ns_vec[...] = slots
    to_smem = pltpu.make_async_copy(ns_vec, ns_smem, small_sem)
    to_smem.start()
    to_smem.wait()

    def source(k):
        src = jnp.int32(0)
        for o in range(8):
            for j in range(4):
                src = jnp.where(ns_smem[o, j] == sess * 4 + k, o, src)
        return src

    sources = [source(k) for k in range(4)]

    steps(START)
    wait_bytes(req3.at[pl.ds(0, 15)], q2_r)
    for i in range(16):
        asked = req3[i]
        for q in range(QCAP):
            col[i * 32 + q * 8:i * 32 + q * 8 + 8, :] = jnp.broadcast_to(asked[:, q:q + 1], (8, 128))
    load_table.wait()
    acc[...] = jnp.zeros(acc.shape, F32)
    depth = 1024

    def look_up(c):
        base = c * depth
        want = col[...] - iota(col.shape, 1) - base
        hot = jnp.concatenate(
            [jnp.where(want == t * 128, 1.0, 0.0).astype(BF) for t in range(depth // 128)], axis=1)
        acc[...] += dot(hot, table[pl.ds(pl.multiple_of(base, depth), depth), :])

    def look_ups(c):
        for slot, names in LOOK.items():
            pl.when(c == slot)(functools.partial(steps, names))
        look_up(c)

    each(0, items // depth, look_ups)
    for i in range(16):
        resp[i] = acc[i * 32:(i + 1) * 32, :].astype(BF)
    back[item] = resp[item]
    each(1, 16, lambda d: response_i(d).start())

    steps(MIDDLE)

    wait_bytes(back.at[pl.ds(0, 15)], p1_r)
    turned[...] = dot(turn[...], back[...].reshape(512, width)).astype(BF).reshape(8, 64, width)
    fetched[sess] = turned[sess]
    each(1, 8, lambda d: response_s(d).start())

    steps(LATER)

    wait_bytes(fetched.at[pl.ds(0, 7)], p2_r)

    def make_cand(g):
        return dot(pick[session_of(g)], fetched[...].reshape(512, width)).astype(BF)

    for g in range(1, 4):
        csend[g] = make_cand(g)
        send_cand(g).start()
    cand[0] = make_cand(0)

    steps(LAST)

    load_wqu.wait()

    def project(r):
        rows = cand[r]
        query[r] = dot(rows, wqu_ref[:, 0:width]).astype(BF)
        g = dot(rows, wqu_ref[:, width:])
        gate[r] = g / (1.0 + jnp.exp(-g))
        mixed[r] = jnp.zeros(mixed.shape[1:], F32)

    wait_bytes(cand.at[pl.ds(1, 3)], c_r)
    each(0, 4, project)

    load_wout.wait()
    head = jnp.broadcast_to(whead_ref[...].astype(F32).reshape(1, width), (16, width)).astype(BF)
    fold = dot_nt(head, wout_ref[...])
    fold0 = fold.astype(BF)
    left = fold - fold0.astype(F32)
    fold1 = left.astype(BF)
    fold2 = (left - fold1.astype(F32)).astype(BF)
    which_row = iota((16, width), 0)
    folds = jnp.where(
        which_row == 0, fold0.astype(F32),
        jnp.where(which_row == 1, fold1.astype(F32), jnp.where(which_row == 2, fold2.astype(F32), 0.0))).astype(BF)
    fold_ref[0] = folds
    fold_ref[1] = jnp.where(which_row == 0, head.astype(F32), 0.0).astype(BF)

    def finish(r):
        m = mixed[r]
        normed = m * lax.rsqrt(jnp.mean(m * m, axis=1, keepdims=True) + 1e-6)
        gated = (normed * gate[r]).astype(BF)
        part = dot_nt(fold_ref[0], gated) + dot_nt(fold_ref[1], cand[r])
        line = jnp.sum(part, axis=0, keepdims=True)
        ssend[r] = jnp.broadcast_to(line, (8, count))

    def attend(p):
        e = 2 * p

        arrive(e)
        arrive(e + 1)
        half = 0.5 / math.sqrt(size)
        spot = iota((1, 8 * span), 1)
        group = lax.rem(spot, 4 * span) // span
        event = (e + spot // (4 * span)) * span + lax.rem(spot, span)
        scales = []
        for m in range(4):
            ax, az = (px if m // 2 else sx), (pz if m % 2 else sz)
            gx = ax + group // 2 * (3 - 2 * ax)
            gz = az + lax.rem(group, 2) * (3 - 2 * az)
            position = device(gx, gz) * (CHUNKS * span) + event
            alive = position < jnp.broadcast_to(len_vec[0:1, 0:1], position.shape)
            scales.append(jnp.where(alive, half, 0.0))

        def rows(r):
            for h in range(HEADS):
                cols = slice(h * size, (h + 1) * size)
                q = query[r, :, cols]
                total = mixed[r, :, cols]
                for m in range(4):
                    keys = kv[pl.ds(e, 2), m, :, 2 * h].reshape(8 * span, size)
                    values = kv[pl.ds(e, 2), m, :, 2 * h + 1].reshape(8 * span, size)
                    u = dot_nt(q, keys) * scales[m]
                    w = (u + u * jnp.tanh(u)).astype(BF)
                    total = total + dot(w, values)
                mixed[r, :, cols] = total

        def turns(n):
            for (slot_p, slot_n), names in LOOP.items():
                pl.when((p == slot_p) & (n == slot_n))(functools.partial(steps, names))
            r = lax.rem(n + 1, 4)
            rows(r)

            @pl.when(p == CHUNKS // 2 - 1)
            def _():
                finish(r)

                @pl.when(r != 0)
                def _():
                    send_score(r).start()

        each(0, 4, turns)

    each(0, CHUNKS // 2, attend)
    sback[0] = ssend[0]

    wait_bytes(req_own.at[pl.ds(0, 112)], q1_s)
    wait_bytes(meta.at[pl.ds(0, 7)], meta_s)
    wait_bytes(req2.at[pl.ds(0, 15)], q2_s)
    wait_bytes(resp.at[pl.ds(0, 15)], p1_s)
    wait_bytes(turned.at[pl.ds(0, 7)], p2_s)
    wait_bytes(csend.at[pl.ds(1, 3)], c_s)
    wait_bytes(sendbuf.at[:, pl.ds(1, 7)], m_s)
    wait_bytes(parted.at[:, pl.ds(0, 3)], z_s)
    wait_bytes(kv.at[:, pl.ds(1, 2)], x_s)
    wait_bytes(kv.at[:, 3], f_s)
    wait_bytes(migbuf, out_sem)
    wait_bytes(ssend.at[pl.ds(1, 3)], o_s)

    wait_bytes(sback.at[pl.ds(1, 3)], o_r)
    for j in range(4):
        line = jnp.zeros((1, count), F32)
        for g in range(4):
            line = jnp.where(session_of(g) == j, sback[g, 0:1, :], line)
        score_out[j:j + 1, :] = line


def hand_on(mig_ref, score_ref, mig_out, score_out, held, in_sem, out_sem):
    parts = 4
    span = mig_ref.shape[1] // parts
    pieces = [(k, pl.ds(t * span, span)) for k in range(mig_ref.shape[0]) for t in range(parts)]
    loads = [
        pltpu.make_async_copy(mig_ref.at[k, part], held.at[k, part], in_sem.at[n])
        for n, (k, part) in enumerate(pieces)]
    stores = [
        pltpu.make_async_copy(held.at[k, part], mig_out.at[k, part], out_sem.at[n])
        for n, (k, part) in enumerate(pieces)]
    for load in loads:
        load.start()
    score_out[...] = score_ref[...]
    for load, store in zip(loads, stores):
        load.wait()
        store.start()
    for store in stores:
        store.wait()


def per_device(cache, lengths, new_slot, unique_ids, inverse, table, w_qu, w_out, w_head):
    sessions, events, _, width = cache.shape
    span = events // CHUNKS
    count = inverse.shape[1]
    size = width // HEADS
    block = 2 * HEADS * span
    whole = cache.reshape(sessions, events, 2, HEADS, size).transpose(0, 1, 3, 2, 4)
    whole = whole.reshape(sessions, events * HEADS * 2, size)
    vm = pl.BlockSpec(memory_space=pltpu.VMEM)
    sm = pl.BlockSpec(memory_space=pltpu.SMEM)
    hb = pl.BlockSpec(memory_space=pl.ANY)
    dma = pltpu.SemaphoreType.DMA
    chunk = (block, size)
    scratch = [
        pltpu.VMEM(whole.shape, BF),
        pltpu.VMEM(w_qu.shape, BF),
        pltpu.VMEM(w_out.shape, BF),
        pltpu.VMEM(table.shape, BF),
        pltpu.VMEM((CHUNKS, 8) + chunk, BF),
        *[pltpu.VMEM((8,) + chunk, BF) for _ in range(CHUNKS)],
        pltpu.VMEM((CHUNKS, 4) + chunk, BF),
        pltpu.VMEM((block, block), BF),
        pltpu.VMEM((CHUNKS, 4, 2 * HEADS, span, size), BF),
        pltpu.VMEM((CHUNKS, 4, 4, 2 * HEADS, span, size), BF),
        pltpu.VMEM((8, 128), I32),
        pltpu.VMEM((8, 8, 128), I32),
        pltpu.VMEM((8, 128), I32),
        pltpu.SMEM((8, 128), I32),
        pltpu.VMEM((8, 128), I32),
        pltpu.VMEM((8, 384), I32),
        pltpu.VMEM((8, count), F32),
        pltpu.VMEM((128, 128), I32),
        pltpu.VMEM((128, 128), I32),
        pltpu.VMEM((16, 8, 128), I32),
        pltpu.VMEM((16, 8, 128), I32),
        pltpu.VMEM((512, 128), I32),
        pltpu.VMEM((512, width), F32),
        pltpu.VMEM((16, 32, width), BF),
        pltpu.VMEM((16, 32, width), BF),
        pltpu.VMEM((8, 64, width), BF),
        pltpu.VMEM((8, 64, width), BF),
        pltpu.VMEM((512, 512), BF),
        pltpu.VMEM((2, 16, width), BF),
        pltpu.VMEM((4, count, 512), BF),
        pltpu.VMEM((4, count, width), BF),
        pltpu.VMEM((4, count, width), BF),
        pltpu.VMEM((4, count, width), BF),
        pltpu.VMEM((4, count, width), F32),
        pltpu.VMEM((4, count, width), F32),
        pltpu.VMEM((4, 8, count), F32),
        pltpu.VMEM((4, 8, count), F32),
        dma, dma, dma, dma, dma, dma,
        dma, dma,
        dma, dma((CHUNKS,)),
        dma, dma((CHUNKS,)),
        dma, dma((CHUNKS,)),
        dma, dma((CHUNKS,)),
        dma, dma, dma, dma,
        dma, dma, dma, dma,
        dma, dma, dma, dma,
    ]
    migrated, scores = pl.pallas_call(
        kernel,
        out_shape=(
            jax.ShapeDtypeStruct(whole.shape, BF),
            jax.ShapeDtypeStruct((sessions, count), F32),
        ),
        in_specs=[sm, sm, vm, vm, hb, hb, hb, hb, vm],
        out_specs=(hb, vm),
        scratch_shapes=scratch,
        compiler_params=pltpu.CompilerParams(
            collective_id=0, has_side_effects=True, vmem_limit_bytes=56 * 1024 * 1024),
        cost_estimate=pl.CostEstimate(flops=12_000_000_000, bytes_accessed=16_000_000, transcendentals=17_000_000),
    )(new_slot, lengths, unique_ids, inverse, whole, table, w_qu, w_out, w_head)
    migrated, scores = pl.pallas_call(
        hand_on,
        out_shape=(
            jax.ShapeDtypeStruct(whole.shape, BF),
            jax.ShapeDtypeStruct((sessions, count), F32),
        ),
        in_specs=[hb, vm],
        out_specs=(hb, vm),
        scratch_shapes=[pltpu.VMEM(whole.shape, BF), dma((16,)), dma((16,))],
    )(migrated, scores)
    migrated = migrated.reshape(sessions, events, HEADS, 2, size).transpose(0, 1, 3, 2, 4)
    return migrated.reshape(cache.shape), scores


def solution(mesh):
    placed = (
        P("session", "item", None, None),
        P("session"),
        P("session"),
        P("session", "item"),
        P("session", "item"),
        P(("session", "item"), None),
        P(),
        P(),
        P(),
    )
    return jax.shard_map(
        per_device,
        mesh=mesh,
        in_specs=placed,
        out_specs=(P("session", "item", None, None), P("session", "item")),
        check_vma=False,
    )
```

```python
import functools
import math

import jax
import jax.numpy as jnp
from jax import lax
from jax.experimental import pallas as pl
from jax.experimental.pallas import tpu as pltpu
from jax.sharding import PartitionSpec as P

HEADS = 4
CHUNKS = 8
AHEAD = 2
ZN = 4
XN = 4
QCAP = 4
START = ("s0", "m2", "s1", "m3")
LOOK = {2: ("x0",), 5: ("x1", "s2", "m4")}
MIDDLE = ("o0", "s3", "m5", "x2", "o1")
LATER = ("s4", "m6", "x3", "o2", "s5", "m7", "x4", "o3")
LAST = ("s6", "x5", "o4")
LOOP = {(0, 0): ("s7", "x6", "o5"), (1, 0): ("x7", "o6"), (2, 0): ("o7",)}
BF = jnp.bfloat16
F32 = jnp.float32
I32 = jnp.int32


def iota(shape, dim):
    return lax.broadcasted_iota(I32, shape, dim)


def dot(a, b):
    return jnp.dot(a, b, preferred_element_type=F32)


def dot_nt(a, b):
    return lax.dot_general(a, b, (((1,), (1,)), ((), ())), preferred_element_type=F32)


def kernel(
    ns_ref, ln_ref, ids_ref, inv_ref, cache_hbm, table_ref, wqu_hbm, wout_hbm, whead_ref,
    mig_out, score_out,
    cache_ref, wqu_ref, wout_ref, table, sendbuf, inc0, inc1, inc2, inc3, inc4, inc5, inc6, inc7, migbuf, split, parted, kv,
    meta_own, meta, ns_vec, ns_smem, len_vec,
    ids_pad, inv_pad, req_own, req1, req2, req3, col, acc, resp, back, turned, fetched,
    turn, fold_ref, pick, csend, cand, query, gate, mixed, ssend, sback,
    cache_sem, wqu_sem, wout_sem, table_sem, small_sem, out_sem,
    meta_s, meta_r, m_s, m_r, z_s, z_r, x_s, x_r, f_s, f_r,
    q1_s, q1_r, q2_s, q2_r, p1_s, p1_r, p2_s, p2_r, c_s, c_r, o_s, o_r,
):
    incoming = (inc0, inc1, inc2, inc3, inc4, inc5, inc6, inc7)
    sess = lax.axis_index("session")
    item = lax.axis_index("item")
    x = item // ZN
    z = item % ZN
    span = kv.shape[4]
    block = 2 * HEADS * span
    width = wout_ref.shape[0]
    size = width // HEADS
    count = inv_ref.shape[1]
    items = table.shape[0]

    def speer(d):
        return lax.rem(sess + d, 8)

    def ipeer(d):
        return lax.rem(item + d, 16)

    core = lax.rem(sess, 2)
    sx = lax.rem(x + XN - core, XN)
    sz = lax.rem(z + ZN - core, ZN)
    px = sx + 1 - 2 * lax.rem(sx, 2)
    pz = sz + 1 - 2 * lax.rem(sz, 2)

    def device(ax, az):
        return lax.rem(ax + core, XN) * ZN + lax.rem(az + core, ZN)

    def mirror(g):
        return sx + g // 2 * (3 - 2 * sx), sz + g % 2 * (3 - 2 * sz)

    def square(ax, az):
        return ax // 2 * 2 + az // 2

    def session_of(g):
        return square(*mirror(g))

    def remote(src, dst, ssem, rsem, s_to, i_to):
        return pltpu.make_async_remote_copy(
            src_ref=src, dst_ref=dst, send_sem=ssem, recv_sem=rsem,
            device_id=(s_to, i_to), device_id_type=pl.DeviceIdType.MESH,
        )

    def each(low, high, body):
        def step(d, carry):
            body(d)
            return carry
        lax.fori_loop(low, high, step, 0)

    def wait_bytes(ref, sem):
        pltpu.make_async_copy(ref, ref, sem).wait()

    load_cache = pltpu.make_async_copy(cache_hbm, cache_ref, cache_sem)
    load_cache.start()
    load_table = pltpu.make_async_copy(table_ref, table, table_sem)
    load_table.start()
    load_wqu = pltpu.make_async_copy(wqu_hbm, wqu_ref, wqu_sem)
    load_wqu.start()
    load_wout = pltpu.make_async_copy(wout_hbm, wout_ref, wout_sem)
    load_wout.start()

    barrier = pltpu.get_barrier_semaphore()

    def greet_session(d):
        pl.semaphore_signal(barrier, inc=1, device_id=(speer(d), item), device_id_type=pl.DeviceIdType.MESH)

    def greet_item(d):
        pl.semaphore_signal(barrier, inc=1, device_id=(sess, ipeer(d)), device_id_type=pl.DeviceIdType.MESH)

    each(1, 8, greet_session)
    each(1, 16, greet_item)

    lanes = ids_pad.shape[1]
    ids_pad[...] = jnp.full(ids_pad.shape, -1, I32)
    ids_pad[0:1, 0:ids_ref.shape[1]] = ids_ref[...]
    ids = ids_pad[0:1, :]
    holder = lax.shift_right_arithmetic(ids, 13)
    row = (ids - holder * items).astype(F32)
    peer = iota((128, lanes), 0)
    member = peer == holder
    ones = jnp.where(member, 1.0, 0.0)
    lower = jnp.where(iota((lanes, lanes), 0) <= iota((lanes, lanes), 1), 1.0, 0.0)
    rank = dot(ones.astype(BF), lower.astype(BF)) * ones
    lane = iota((128, 128), 1)
    wanted = jnp.zeros((128, 128), F32)
    for q in range(QCAP):
        one = jnp.sum(jnp.where(rank == q + 1.0, row, 0.0), axis=1, keepdims=True)
        wanted = jnp.where(lane == q, one, wanted)
    req_own[...] = wanted.astype(I32)
    place = jnp.sum(jnp.where(member, (peer * QCAP).astype(F32) + rank - 1.0, 0.0), axis=0, keepdims=True)

    meta_lane = iota((8, 128), 1)
    meta_row = iota((8, 128), 0)
    mine = jnp.zeros((8, 128), I32)
    for j in range(4):
        both = jnp.where(meta_row == 0, ns_ref[j], ln_ref[j])
        mine = jnp.where(meta_lane == j, both, mine)
    mine = jnp.where(meta_lane < 4, mine, -1)
    meta_own[...] = mine
    meta[sess] = mine

    def fill(e, d):
        to = speer(d)
        which = jnp.int32(0)
        for j in range(4):
            which = jnp.where(lax.shift_right_arithmetic(ns_ref[j], 2) == to, j, which)
        return cache_ref[which, e * block:(e + 1) * block, :]

    def prepare(e):
        def body(d):
            sendbuf[e, d] = fill(e, d)
        incoming[e][sess] = fill(e, 0)
        each(1, 8, body)

    def migrate(e, d):
        return remote(sendbuf.at[e, d], incoming[e].at[sess], m_s, m_r.at[e], speer(d), item)

    def request_s(d):
        to = speer(d)
        return remote(
            req_own.at[pl.ds(pl.multiple_of(to * 16, 16), 16)],
            req1.at[pl.ds(pl.multiple_of(sess * 16, 16), 16)],
            q1_s, q1_r, to, item)

    def request_i(d):
        to = ipeer(d)
        return remote(req2.at[to], req3.at[item], q2_s, q2_r, sess, to)

    def response_i(d):
        to = ipeer(d)
        return remote(resp.at[to], back.at[item], p1_s, p1_r, sess, to)

    def response_s(d):
        to = speer(d)
        return remote(turned.at[to], fetched.at[sess], p2_s, p2_r, to, item)

    def tell(d):
        return remote(meta_own, meta.at[sess], meta_s, meta_r, speer(d), item)

    def enter(e, g):
        return remote(
            parted.at[e, session_of(g)], kv.at[e, 0, g], z_s, z_r.at[e], sess, device(*mirror(g)))

    def pair(e, way):
        to = device(px, sz) if way == 0 else device(sx, pz)
        return remote(kv.at[e, 0], kv.at[e, 2 if way == 0 else 1], x_s, x_r.at[e], sess, to)

    def across(e, way):
        to = device(sx, pz) if way == 0 else device(px, sz)
        part = pl.ds(0, 2) if way == 0 else pl.ds(2, 2)
        return remote(
            kv.at[e, 2 if way == 0 else 1, part], kv.at[e, 3, part], f_s, f_r.at[e], sess, to)

    def send_cand(g):
        return remote(csend.at[g], cand.at[g], c_s, c_r, sess, device(*mirror(g)))

    def send_score(g):
        return remote(ssend.at[g], sback.at[g], o_s, o_r, sess, device(*mirror(g)))

    def settle(e):
        wait_bytes(incoming[e].at[pl.ds(0, 7)], m_r.at[e])
        for k in range(4):
            rows = incoming[e][sources[k]]
            migbuf[e, k] = rows
            parted[e, k] = dot(split[...], rows).astype(BF).reshape(2 * HEADS, span, size)
        each(1, 4, lambda g: enter(e, g).start())
        kv[e, 0, 0] = parted[e, session_of(0)]
        store_out(e).start()

    def spread(e):
        wait_bytes(kv.at[e, 0, pl.ds(0, 3)], z_r.at[e])
        for way in range(2):
            pair(e, way).start()

    def onward(e):
        wait_bytes(kv.at[e, pl.ds(1, 2)], x_r.at[e])
        for way in range(2):
            across(e, way).start()

    def arrive(e):
        wait_bytes(kv.at[e, 3], f_r.at[e])

    def store_out(e):
        return pltpu.make_async_copy(migbuf.at[e], mig_out.at[:, pl.ds(e * block, block), :], out_sem)

    def launch(e):
        if e >= AHEAD:
            prepare(e)
        each(1, 8, lambda d: migrate(e, d).start())

    def steps(names):
        for name in names:
            {"m": launch, "s": settle, "x": spread, "o": onward}[name[0]](int(name[1:]))

    load_cache.wait()
    for e in range(AHEAD):
        prepare(e)
    pl.semaphore_wait(barrier, 22)
    each(1, 8, lambda d: request_s(d).start())
    each(1, 8, lambda d: tell(d).start())
    for e in range(AHEAD):
        launch(e)
    own = pl.ds(pl.multiple_of(sess * 16, 16), 16)
    req1[own] = req_own[own]

    to_row = iota((block, block), 0)
    from_row = lax.rem(to_row, span) * (2 * HEADS) + to_row // span
    split[...] = jnp.where(from_row == iota((block, block), 1), 1.0, 0.0).astype(BF)
    put = jnp.where(iota((512, lanes), 0).astype(F32) == place, 1.0, 0.0).astype(BF)
    inv_pad[...] = jnp.zeros(inv_pad.shape, F32)
    inv_pad[0:4, :] = inv_ref[...].astype(F32)
    inv_col = jnp.transpose(inv_pad[...])
    for j in range(4):
        hot = jnp.where(iota((count, lanes), 1).astype(F32) == inv_col[:, j:j + 1], 1.0, 0.0).astype(BF)
        pick[j] = dot_nt(hot, put).astype(BF)
    out_row = iota((512, 512), 0)
    in_row = lax.rem(out_row, 64) // 4 * 32 + lax.rem(out_row, 4) * 8 + out_row // 64
    turn[...] = jnp.where(in_row == iota((512, 512), 1), 1.0, 0.0).astype(BF)

    wait_bytes(req1.at[pl.ds(0, 112)], q1_r)
    for i in range(16):
        req2[i] = req1[pl.ds(i, 8, stride=16), :]
    req3[item] = req2[item]
    each(1, 16, lambda d: request_i(d).start())

    wait_bytes(meta.at[pl.ds(0, 7)], meta_r)
    slots = jnp.zeros((8, 128), I32)
    live = jnp.zeros((1, 128), I32)
    for o in range(8):
        first = meta[o, 0:1, :]
        slots = jnp.where(meta_row == o, first, slots)
        live = live + jnp.where(first == sess * 4 + session_of(0), meta[o, 1:2, :], 0)
    live = jnp.sum(live.astype(F32), axis=1, keepdims=True)
    len_vec[...] = jnp.broadcast_to(live, (8, 128)).astype(I32)
    ns_vec[...] = slots
    to_smem = pltpu.make_async_copy(ns_vec, ns_smem, small_sem)
    to_smem.start()
    to_smem.wait()

    def source(k):
        src = jnp.int32(0)
        for o in range(8):
            for j in range(4):
                src = jnp.where(ns_smem[o, j] == sess * 4 + k, o, src)
        return src

    sources = [source(k) for k in range(4)]

    steps(START)
    wait_bytes(req3.at[pl.ds(0, 15)], q2_r)
    for i in range(16):
        asked = req3[i]
        for q in range(QCAP):
            col[i * 32 + q * 8:i * 32 + q * 8 + 8, :] = jnp.broadcast_to(asked[:, q:q + 1], (8, 128))
    load_table.wait()
    acc[...] = jnp.zeros(acc.shape, F32)
    depth = 1024

    def look_up(c):
        base = c * depth
        want = col[...] - iota(col.shape, 1) - base
        hot = jnp.concatenate(
            [jnp.where(want == t * 128, 1.0, 0.0).astype(BF) for t in range(depth // 128)], axis=1)
        acc[...] += dot(hot, table[pl.ds(pl.multiple_of(base, depth), depth), :])

    def look_ups(c):
        for slot, names in LOOK.items():
            pl.when(c == slot)(functools.partial(steps, names))
        look_up(c)

    each(0, items // depth, look_ups)
    for i in range(16):
        resp[i] = acc[i * 32:(i + 1) * 32, :].astype(BF)
    back[item] = resp[item]
    each(1, 16, lambda d: response_i(d).start())

    steps(MIDDLE)

    wait_bytes(back.at[pl.ds(0, 15)], p1_r)
    turned[...] = dot(turn[...], back[...].reshape(512, width)).astype(BF).reshape(8, 64, width)
    fetched[sess] = turned[sess]
    each(1, 8, lambda d: response_s(d).start())

    steps(LATER)

    wait_bytes(fetched.at[pl.ds(0, 7)], p2_r)

    def make_cand(g):
        return dot(pick[session_of(g)], fetched[...].reshape(512, width)).astype(BF)

    for g in range(1, 4):
        csend[g] = make_cand(g)
        send_cand(g).start()
    cand[0] = make_cand(0)

    steps(LAST)

    load_wqu.wait()

    def project(r):
        rows = cand[r]
        query[r] = dot(rows, wqu_ref[:, 0:width]).astype(BF)
        g = dot(rows, wqu_ref[:, width:])
        gate[r] = g / (1.0 + jnp.exp(-g))
        mixed[r] = jnp.zeros(mixed.shape[1:], F32)

    project(0)

    load_wout.wait()
    head = jnp.broadcast_to(whead_ref[...].astype(F32).reshape(1, width), (16, width)).astype(BF)
    fold = dot_nt(head, wout_ref[...])
    fold0 = fold.astype(BF)
    left = fold - fold0.astype(F32)
    fold1 = left.astype(BF)
    fold2 = (left - fold1.astype(F32)).astype(BF)
    which_row = iota((16, width), 0)
    folds = jnp.where(
        which_row == 0, fold0.astype(F32),
        jnp.where(which_row == 1, fold1.astype(F32), jnp.where(which_row == 2, fold2.astype(F32), 0.0))).astype(BF)
    fold_ref[0] = folds
    fold_ref[1] = jnp.where(which_row == 0, head.astype(F32), 0.0).astype(BF)

    wait_bytes(cand.at[pl.ds(1, 3)], c_r)
    each(1, 4, project)


    def finish(r):
        m = mixed[r]
        normed = m * lax.rsqrt(jnp.mean(m * m, axis=1, keepdims=True) + 1e-6)
        gated = (normed * gate[r]).astype(BF)
        part = dot_nt(fold_ref[0], gated) + dot_nt(fold_ref[1], cand[r])
        line = jnp.sum(part, axis=0, keepdims=True)
        ssend[r] = jnp.broadcast_to(line, (8, count))

    def attend(p):
        e = 2 * p

        arrive(e)
        arrive(e + 1)
        half = 0.5 / math.sqrt(size)
        spot = iota((1, 8 * span), 1)
        group = lax.rem(spot, 4 * span) // span
        event = (e + spot // (4 * span)) * span + lax.rem(spot, span)
        scales = []
        for m in range(4):
            ax, az = (px if m // 2 else sx), (pz if m % 2 else sz)
            gx = ax + group // 2 * (3 - 2 * ax)
            gz = az + lax.rem(group, 2) * (3 - 2 * az)
            position = device(gx, gz) * (CHUNKS * span) + event
            alive = position < jnp.broadcast_to(len_vec[0:1, 0:1], position.shape)
            scales.append(jnp.where(alive, half, 0.0))

        def rows(r):
            for h in range(HEADS):
                cols = slice(h * size, (h + 1) * size)
                q = query[r, :, cols]
                total = mixed[r, :, cols]
                for m in range(4):
                    keys = kv[pl.ds(e, 2), m, :, 2 * h].reshape(8 * span, size)
                    values = kv[pl.ds(e, 2), m, :, 2 * h + 1].reshape(8 * span, size)
                    u = dot_nt(q, keys) * scales[m]
                    w = (u + u * jnp.tanh(u)).astype(BF)
                    total = total + dot(w, values)
                mixed[r, :, cols] = total

        def turns(n):
            for (slot_p, slot_n), names in LOOP.items():
                pl.when((p == slot_p) & (n == slot_n))(functools.partial(steps, names))
            r = lax.rem(n + 1, 4)
            rows(r)

            @pl.when(p == CHUNKS // 2 - 1)
            def _():
                finish(r)

                @pl.when(r != 0)
                def _():
                    send_score(r).start()

        each(0, 4, turns)

    each(0, CHUNKS // 2, attend)
    sback[0] = ssend[0]

    wait_bytes(req_own.at[pl.ds(0, 112)], q1_s)
    wait_bytes(meta.at[pl.ds(0, 7)], meta_s)
    wait_bytes(req2.at[pl.ds(0, 15)], q2_s)
    wait_bytes(resp.at[pl.ds(0, 15)], p1_s)
    wait_bytes(turned.at[pl.ds(0, 7)], p2_s)
    wait_bytes(csend.at[pl.ds(1, 3)], c_s)
    wait_bytes(sendbuf.at[:, pl.ds(1, 7)], m_s)
    wait_bytes(parted.at[:, pl.ds(0, 3)], z_s)
    wait_bytes(kv.at[:, pl.ds(1, 2)], x_s)
    wait_bytes(kv.at[:, 3], f_s)
    wait_bytes(migbuf, out_sem)
    wait_bytes(ssend.at[pl.ds(1, 3)], o_s)

    wait_bytes(sback.at[pl.ds(1, 3)], o_r)
    for j in range(4):
        line = jnp.zeros((1, count), F32)
        for g in range(4):
            line = jnp.where(session_of(g) == j, sback[g, 0:1, :], line)
        score_out[j:j + 1, :] = line


def hand_on(mig_ref, score_ref, mig_out, score_out, held, in_sem, out_sem):
    parts = 4
    span = mig_ref.shape[1] // parts
    pieces = [(k, pl.ds(t * span, span)) for k in range(mig_ref.shape[0]) for t in range(parts)]
    loads = [
        pltpu.make_async_copy(mig_ref.at[k, part], held.at[k, part], in_sem.at[n])
        for n, (k, part) in enumerate(pieces)]
    stores = [
        pltpu.make_async_copy(held.at[k, part], mig_out.at[k, part], out_sem.at[n])
        for n, (k, part) in enumerate(pieces)]
    for load in loads:
        load.start()
    score_out[...] = score_ref[...]
    for load, store in zip(loads, stores):
        load.wait()
        store.start()
    for store in stores:
        store.wait()


def per_device(cache, lengths, new_slot, unique_ids, inverse, table, w_qu, w_out, w_head):
    sessions, events, _, width = cache.shape
    span = events // CHUNKS
    count = inverse.shape[1]
    size = width // HEADS
    block = 2 * HEADS * span
    whole = cache.reshape(sessions, events, 2, HEADS, size).transpose(0, 1, 3, 2, 4)
    whole = whole.reshape(sessions, events * HEADS * 2, size)
    vm = pl.BlockSpec(memory_space=pltpu.VMEM)
    sm = pl.BlockSpec(memory_space=pltpu.SMEM)
    hb = pl.BlockSpec(memory_space=pl.ANY)
    dma = pltpu.SemaphoreType.DMA
    chunk = (block, size)
    scratch = [
        pltpu.VMEM(whole.shape, BF),
        pltpu.VMEM(w_qu.shape, BF),
        pltpu.VMEM(w_out.shape, BF),
        pltpu.VMEM(table.shape, BF),
        pltpu.VMEM((CHUNKS, 8) + chunk, BF),
        *[pltpu.VMEM((8,) + chunk, BF) for _ in range(CHUNKS)],
        pltpu.VMEM((CHUNKS, 4) + chunk, BF),
        pltpu.VMEM((block, block), BF),
        pltpu.VMEM((CHUNKS, 4, 2 * HEADS, span, size), BF),
        pltpu.VMEM((CHUNKS, 4, 4, 2 * HEADS, span, size), BF),
        pltpu.VMEM((8, 128), I32),
        pltpu.VMEM((8, 8, 128), I32),
        pltpu.VMEM((8, 128), I32),
        pltpu.SMEM((8, 128), I32),
        pltpu.VMEM((8, 128), I32),
        pltpu.VMEM((8, 384), I32),
        pltpu.VMEM((8, count), F32),
        pltpu.VMEM((128, 128), I32),
        pltpu.VMEM((128, 128), I32),
        pltpu.VMEM((16, 8, 128), I32),
        pltpu.VMEM((16, 8, 128), I32),
        pltpu.VMEM((512, 128), I32),
        pltpu.VMEM((512, width), F32),
        pltpu.VMEM((16, 32, width), BF),
        pltpu.VMEM((16, 32, width), BF),
        pltpu.VMEM((8, 64, width), BF),
        pltpu.VMEM((8, 64, width), BF),
        pltpu.VMEM((512, 512), BF),
        pltpu.VMEM((2, 16, width), BF),
        pltpu.VMEM((4, count, 512), BF),
        pltpu.VMEM((4, count, width), BF),
        pltpu.VMEM((4, count, width), BF),
        pltpu.VMEM((4, count, width), BF),
        pltpu.VMEM((4, count, width), F32),
        pltpu.VMEM((4, count, width), F32),
        pltpu.VMEM((4, 8, count), F32),
        pltpu.VMEM((4, 8, count), F32),
        dma, dma, dma, dma, dma, dma,
        dma, dma,
        dma, dma((CHUNKS,)),
        dma, dma((CHUNKS,)),
        dma, dma((CHUNKS,)),
        dma, dma((CHUNKS,)),
        dma, dma, dma, dma,
        dma, dma, dma, dma,
        dma, dma, dma, dma,
    ]
    migrated, scores = pl.pallas_call(
        kernel,
        out_shape=(
            jax.ShapeDtypeStruct(whole.shape, BF),
            jax.ShapeDtypeStruct((sessions, count), F32),
        ),
        in_specs=[sm, sm, vm, vm, hb, hb, hb, hb, vm],
        out_specs=(hb, vm),
        scratch_shapes=scratch,
        compiler_params=pltpu.CompilerParams(
            collective_id=0, has_side_effects=True, vmem_limit_bytes=56 * 1024 * 1024),
        cost_estimate=pl.CostEstimate(flops=12_000_000_000, bytes_accessed=16_000_000, transcendentals=17_000_000),
    )(new_slot, lengths, unique_ids, inverse, whole, table, w_qu, w_out, w_head)
    migrated, scores = pl.pallas_call(
        hand_on,
        out_shape=(
            jax.ShapeDtypeStruct(whole.shape, BF),
            jax.ShapeDtypeStruct((sessions, count), F32),
        ),
        in_specs=[hb, vm],
        out_specs=(hb, vm),
        scratch_shapes=[pltpu.VMEM(whole.shape, BF), dma((16,)), dma((16,))],
    )(migrated, scores)
    migrated = migrated.reshape(sessions, events, HEADS, 2, size).transpose(0, 1, 3, 2, 4)
    return migrated.reshape(cache.shape), scores


def solution(mesh):
    placed = (
        P("session", "item", None, None),
        P("session"),
        P("session"),
        P("session", "item"),
        P("session", "item"),
        P(("session", "item"), None),
        P(),
        P(),
        P(),
    )
    return jax.shard_map(
        per_device,
        mesh=mesh,
        in_specs=placed,
        out_specs=(P("session", "item", None, None), P("session", "item")),
        check_vma=False,
    )
```
